32 devices in a mesh: head: 4 (over z), ctx: 8 (over y, x, core).
Axes of the slice: x: 2, y: 2, z: 4, core: 2. Of those that a mesh axis runs over, the one named last changes fastest.
Arguments:
- q_latent: bfloat16 [1024, 64, 512], P('ctx', 'head'), may hold values from -128 to 128
- q_rope: bfloat16 [1024, 64, 64], P('ctx', 'head'), may hold values from -6 to 6
- latent: bfloat16 [1024, 512], P('ctx'), may hold values from -10 to 10
- rope_key: bfloat16 [1024, 64], P('ctx'), may hold values from -6 to 6
- positions: int32 [1024], replicated, may hold values from 0 to 1023, as said below
- d_out: bfloat16 [1024, 64, 128], P('ctx', 'head'), may hold values from -6 to 6
- w_uv: bfloat16 [64, 512, 128], P('head'), may hold values from -0.25 to 0.25
Outputs:
- d_q_latent: bfloat16 [1024, 64, 512], P('ctx', 'head')
- d_q_rope: bfloat16 [1024, 64, 64], P('ctx', 'head')
- d_latent: float32 [1024, 512], P(('head', 'ctx'))
- d_rope_key: float32 [1024, 64], P(('head', 'ctx'))
The draws below stay inside these ranges and needn't reach their ends.
Inputs may be any that keep to these rules, and one draw needn't show every extreme that they name: A permutation of the positions of the prompt, made of aligned runs of 64 tokens (tokens k * 64 onward) that hold consecutive positions in increasing order; the order of the runs is arbitrary.
All inputs are finite; a program needn't handle non-finite values.
Results may differ from the reference program's by a relative error of at most 0.007.
Values may be sent and summed in bfloat16 or wider, within the bound.
No kernel may reach another device: no remote copies, remote signals or barrier semaphores. Data moves between devices by JAX's collectives and lax.ppermute only.
A program may use at most 64 MiB of HBM per device.

```python
import jax
import jax.numpy as jnp
from jax import lax

HEADS = 64
KV_RANK = 512
ROPE = 64
NOPE = 128
VHEAD = 128
TOK_DEV = 128
SEQ = 1024


def latent_bases(key):
    first_base = jnp.clip(jax.random.normal(jax.random.fold_in(key, 501), (SEQ, KV_RANK), jnp.float32), -5.0, 5.0)
    return first_base


def draw_latent(key, part):
    first_base = latent_bases(key)
    return first_base.astype(jnp.bfloat16)


def draw_q_latent(key, part):
    key = jax.random.fold_in(key, 12)
    queries = jax.random.normal(key, (SEQ, HEADS, KV_RANK), jnp.float32)
    return queries.astype(jnp.bfloat16)


def draw_positions(key, part):
    key = jax.random.fold_in(key, 13)
    run_rows = TOK_DEV // 2
    order = jax.random.permutation(key, SEQ // run_rows)
    row_index = jnp.arange(SEQ)
    return (order[row_index // run_rows] * run_rows + row_index % run_rows).astype(jnp.int32)


def block_scale(rng, extent, pieces, low, top_value):
    factor_of, own = 1.0, jax.random.fold_in(rng, 6)
    for position, blocks in pieces:
        steps = jnp.exp(jax.random.uniform(jax.random.fold_in(own, position), (blocks,), jnp.float32, low / len(pieces), top_value / len(pieces)))
        factor_of = factor_of * jnp.repeat(steps, extent[position] // blocks).reshape([-1 if axis == position else 1 for axis in range(len(extent))])
    return factor_of


def noise(key, dims, deviation, reach, cuts=(), kind=jnp.bfloat16):
    values = jax.random.normal(key, dims, jnp.float32) * deviation
    if len(cuts) > 0:
        values = block_scale(key, dims, cuts, -0.22, 0.18) * values
    return jnp.clip(values, min=-reach, max=reach).astype(kind)


def setup_inputs(seed: int = 0) -> dict:
    keys = jax.random.split(jax.random.key(seed), 8)
    return {
        "q_latent": draw_q_latent(jax.random.fold_in(keys[7], 71), 0),
        "q_rope": noise(keys[1], (SEQ, HEADS, ROPE), 1.0, 6.0, ((0, 8), (1, 4))),
        "latent": draw_latent(jax.random.fold_in(keys[7], 71), 0),
        "rope_key": noise(keys[3], (SEQ, ROPE), 1.0, 6.0, ((0, 8),)),
        "positions": draw_positions(jax.random.fold_in(keys[7], 71), 0),
        "d_out": noise(keys[5], (SEQ, HEADS, VHEAD), 1.0, 6.0, ((0, 8), (1, 4))),
        "w_uv": noise(keys[6], (HEADS, KV_RANK, VHEAD), KV_RANK ** -0.5, 0.25, ((0, 4),)),
    }


ROPE_BASE = 10000.0


def rotate(values, places, direction):
    middle = values.shape[-1] // 2
    inverse = ROPE_BASE ** (-(jnp.arange(middle, dtype=jnp.float32) / middle))
    angles = places.astype(jnp.float32)[:, None] * inverse[None, :]
    cosine = jnp.concatenate([jnp.cos(angles), jnp.cos(angles)], -1)
    sine_table = jnp.concatenate([jnp.sin(angles), jnp.sin(angles)], -1)
    if values.ndim == 3:
        cosine = cosine[:, None, :]
        sine_table = sine_table[:, None, :]
    turned = jnp.concatenate([-values[..., middle:], values[..., :middle]], -1)
    return values * cosine + direction * turned * sine_table


def reference(q_latent, q_rope, latent, rope_key, positions, d_out, w_uv):
    scaling = (NOPE + ROPE) ** -0.5
    rank_width = latent.shape[1]
    rope_width = rope_key.shape[1]
    q_turned = rotate(q_rope.astype(jnp.float32), positions, 1.0).astype(jnp.bfloat16)
    k_turned = rotate(rope_key.astype(jnp.float32), positions, 1.0).astype(jnp.bfloat16)
    out_latent = jnp.einsum("shv,hcv->shc", d_out.astype(jnp.float32), w_uv.astype(jnp.float32)).astype(jnp.bfloat16)
    key_rows = jnp.concatenate([latent, k_turned], -1)
    query_rows = jnp.concatenate([q_latent, q_turned], -1)
    visible = positions[None, :] <= positions[:, None]

    def one_head(summed, inputs):
        queries, gradients = inputs
        scores = jnp.dot(queries, key_rows.T, preferred_element_type=jnp.float32) * scaling
        scores = jnp.where(visible, scores, -jnp.inf)
        largest = jnp.max(scores, axis=1, keepdims=True)
        weights = jnp.exp(scores - largest)
        weights = weights / jnp.sum(weights, axis=1, keepdims=True)
        upstream = jnp.dot(gradients, latent.T, preferred_element_type=jnp.float32)
        diagonal_term = jnp.sum(weights * upstream, axis=1, keepdims=True)
        score_grad = (weights * (upstream - diagonal_term) * scaling).astype(jnp.bfloat16)
        weights_low = weights.astype(jnp.bfloat16)
        query_grad = jnp.dot(score_grad, key_rows, preferred_element_type=jnp.float32)
        key_grad = jnp.dot(score_grad.T, queries, preferred_element_type=jnp.float32)
        value_grad = jnp.dot(weights_low.T, gradients, preferred_element_type=jnp.float32)
        padding = jnp.zeros((value_grad.shape[0], rope_width), jnp.float32)
        key_grad = key_grad + jnp.concatenate([value_grad, padding], 1)
        return summed + key_grad, (query_grad[:, :rank_width].astype(jnp.bfloat16), query_grad[:, rank_width:])

    initial = jnp.zeros((positions.shape[0], rank_width + rope_width), jnp.float32)
    summed, (latent_grads, rope_grads) = lax.scan(
        one_head, initial, (jnp.swapaxes(query_rows, 0, 1), jnp.swapaxes(out_latent, 0, 1)))
    d_q_latent = jnp.swapaxes(latent_grads, 0, 1)
    d_q_rope = rotate(jnp.swapaxes(rope_grads, 0, 1), positions, -1.0).astype(jnp.bfloat16)
    d_latent = summed[:, :rank_width]
    d_rope_key = rotate(summed[:, rank_width:], positions, -1.0)
    return (d_q_latent, d_q_rope, d_latent, d_rope_key)
```

```python
import functools
import math

import jax
import jax.numpy as jnp
import numpy as np
from jax import lax
from jax.experimental import pallas as pl
from jax.experimental.pallas import tpu as pltpu
from jax.sharding import PartitionSpec as P

NOPE = 128
RUN = 64
TILE = 256
STEP = 128
ROPE_BASE = 10000.0
NEGATIVE = -1e30
MIB = 1 << 20
BF16 = jnp.bfloat16
F32 = jnp.float32


def dot_nn(left, right):
    return lax.dot_general(left, right, (((1,), (0,)), ((), ())), preferred_element_type=F32)


def dot_nt(left, right):
    return lax.dot_general(left, right, (((1,), (1,)), ((), ())), preferred_element_type=F32)


def dot_tn(left, right):
    return lax.dot_general(left, right, (((0,), (0,)), ((), ())), preferred_element_type=F32)


def half_turn(values):
    middle = values.shape[-1] // 2
    return jnp.concatenate([-values[..., middle:], values[..., :middle]], -1)


def vmem():
    return pl.BlockSpec(memory_space=pltpu.VMEM)


def smem():
    return pl.BlockSpec(memory_space=pltpu.SMEM)


def whole(shape):
    return pl.BlockSpec(shape, lambda *_: (0,) * len(shape))


def params(mib):
    return pltpu.CompilerParams(vmem_limit_bytes=mib * MIB)


def key_kernel(head_axis, ctx_axis, places, latent, rope, inverse, keys, cosine, sine, out_cosine, out_sine):
    me = lax.axis_index("ctx")
    tokens, rank = latent.shape
    for run in range(tokens // RUN):
        rows = pl.ds(run * RUN, RUN)
        first = places[me * tokens + run * RUN]
        count = lax.broadcasted_iota(jnp.int32, (RUN, rope.shape[1]), 0) + first
        angles = count.astype(F32) * inverse[...]
        cosine[rows, :] = jnp.cos(angles)
        sine[rows, :] = jnp.sin(angles)
    out_rows = out_cosine.shape[0]
    block = lax.axis_index("head") * ctx_axis + me
    first = places[block * out_rows]
    count = lax.broadcasted_iota(jnp.int32, out_cosine.shape, 0) + first
    angles = count.astype(F32) * inverse[...]
    out_cosine[...] = jnp.cos(angles)
    out_sine[...] = jnp.sin(angles)
    values = rope[...].astype(F32)
    turned = values * cosine[...] + half_turn(values) * sine[...]
    keys[:, :rank] = latent[...]
    keys[:, rank:] = turned.astype(BF16)


def query_kernel(heads, q_latent, q_rope, cosine, sine, d_out, w_uv, queries, grads, by_head, grad_heads):
    rows, rank = q_latent.shape
    rope = q_rope.shape[1]
    span = TILE // heads
    shift_span, shift_heads = span.bit_length() - 1, heads.bit_length() - 1
    by_row = lax.broadcasted_iota(jnp.int32, (TILE, TILE), 0)
    by_column = lax.broadcasted_iota(jnp.int32, (TILE, TILE), 1)
    same = ((by_row >> shift_span) == (by_column & (heads - 1))) & (
        (by_row & (span - 1)) == (by_column >> shift_heads)
    )
    to_heads = jnp.where(same, 1.0, 0.0).astype(BF16)
    tiles = rows // TILE
    queries[:, :rank] = q_latent[...]
    queries[:, rank + rope :] = jnp.zeros((rows, queries.shape[1] - rank - rope), BF16)
    for tile in range(tiles):
        here = slice(tile * TILE, (tile + 1) * TILE)
        own = slice(tile * span, (tile + 1) * span)
        values = q_rope[here, :].astype(F32)
        spread = lambda table: jnp.broadcast_to(table[own, :][:, None, :], (span, heads, rope)).reshape(TILE, rope)
        turned = values * spread(cosine) + half_turn(values) * spread(sine)
        queries[here, rank : rank + rope] = turned.astype(BF16)
        by_head[:, own, :] = dot_nn(to_heads, d_out[here, :]).astype(BF16).reshape(heads, span, d_out.shape[1])
    for head in range(heads):
        grad_heads[head] = dot_nt(by_head[head], w_uv[head]).astype(BF16)
    for tile in range(tiles):
        here = slice(tile * TILE, (tile + 1) * TILE)
        own = slice(tile * span, (tile + 1) * span)
        block = grad_heads[:, own, :].reshape(TILE, rank)
        grads[here, :] = dot_tn(to_heads, block).astype(BF16)


def place_rows(places, total, out, core, ctx_axis):
    out_rows, width = out.shape[2], out.shape[3]
    chip = lax.axis_index("ctx") >> 1
    half_run = RUN // 2
    for run in range(places.shape[0] // RUN):
        rank_of_run = places[run * RUN] // RUN
        for piece in range(half_run // out_rows):
            block = run * (RUN // out_rows) + 2 * piece
            source = pl.ds(pl.multiple_of(rank_of_run * half_run + piece * out_rows, out_rows), out_rows)
            slot = ((block % ctx_axis) >> 1) ^ chip
            out[slot, block // ctx_axis] = total[source, :width].astype(out.dtype)


def front_kernel(ctx_axis, heads, tokens, out_rows, scaling, places, *refs):
    blocks = refs[:ctx_axis]
    queries, grads, sent, keys, weights_kept, score_grads, weights_sent, total, scores, upstream = refs[ctx_axis:]
    step = pl.program_id(0)
    me = lax.axis_index("ctx")
    core = me & 1
    half_run = RUN // 2
    half = keys.shape[1]
    rank = grads.shape[1]
    width = blocks[0].shape[1]
    rows = queries.shape[0]

    @pl.when(step == 0)
    def _():
        total[...] = jnp.zeros_like(total)
        keys[:, :, width:] = jnp.zeros((2, half, keys.shape[2] - width), BF16)
        for far in range(ctx_axis):
            for run in range(tokens // RUN):
                rank_of_run = places[(me ^ far) * tokens + run * RUN] // RUN
                for sub in range(RUN // out_rows):
                    group = (core ^ (sub & 1)) ^ 1
                    start = pl.multiple_of(rank_of_run * half_run + (sub // 2) * out_rows, out_rows)
                    piece = blocks[far][run * RUN + sub * out_rows : run * RUN + (sub + 1) * out_rows, :]
                    keys[group, pl.ds(start, out_rows), :width] = piece

    first = places[me * tokens + step * RUN]
    visible_steps = ((first // RUN) * half_run) // STEP + 1

    def run_of_queries(steps):
        seen = steps * STEP
        for tile in range(rows // TILE):
            here = slice(tile * TILE, (tile + 1) * TILE)
            score, up = scores.at[tile % 2], upstream.at[tile % 2]
            tile_queries = queries[here, :]
            tile_grads = grads[here, :]
            lanes = lax.broadcasted_iota(jnp.int32, (1, TILE), 1)
            query_places = first + ((lanes + tile * TILE) >> (heads.bit_length() - 1))
            peak = jnp.full((8, TILE), NEGATIVE, F32)
            for group in range(2):
                for part in range(steps):
                    at = slice(group * seen + part * STEP, group * seen + (part + 1) * STEP)
                    value = dot_nt(keys[group, part * STEP : (part + 1) * STEP, :], tile_queries)
                    if part == steps - 1:
                        index = lax.broadcasted_iota(jnp.int32, (STEP, 1), 0) + part * STEP
                        bit = core ^ (1 - group)
                        key_places = index + (index & ~(out_rows - 1)) + bit * out_rows
                        value = jnp.where(key_places <= query_places, value, NEGATIVE)
                    score[at, :] = value
                    peak = jnp.maximum(peak, jnp.max(value.reshape(STEP // 8, 8, TILE), axis=0))
                    up[at, :] = dot_nt(keys[group, part * STEP : (part + 1) * STEP, :rank], tile_grads)
            factor = scaling * math.log2(math.e)
            peak = jnp.max(peak, axis=0, keepdims=True) * factor
            sums = jnp.zeros((8, TILE), F32)
            mixed = jnp.zeros((8, TILE), F32)
            piece = 64
            for part in range(2 * seen // piece):
                at = slice(part * piece, (part + 1) * piece)
                value = jnp.exp2(score[at, :] * factor - peak)
                score[at, :] = value
                sums += jnp.sum(value.reshape(piece // 8, 8, TILE), axis=0)
                mixed += jnp.sum((value * up[at, :]).reshape(piece // 8, 8, TILE), axis=0)
            inverse = 1.0 / jnp.sum(sums, axis=0, keepdims=True)
            diagonal = jnp.sum(mixed, axis=0, keepdims=True) * inverse
            scaled = inverse * scaling
            for part in range(2 * seen // piece):
                at = slice(part * piece, (part + 1) * piece)
                group, row = (part * piece) // seen, (part * piece) % seen
                to = slice(row, row + piece)
                value = score[at, :]
                weight = (value * inverse).astype(BF16)
                if group == 0:
                    weights_sent[to, here] = weight
                else:
                    weights_kept[0, to, here] = weight
                grad = (value * scaled) * (up[at, :] - diagonal)
                score_grads[0, group, to, here] = grad.astype(BF16)
        total[:seen, :] += dot_nn(score_grads[0, 0, :seen, :], queries[...])
        total[:seen, :rank] += dot_nn(weights_sent[:seen, :], grads[...])

    for steps in range(1, half // STEP + 1):
        pl.when(visible_steps == steps)(functools.partial(run_of_queries, steps))

    @pl.when(step == pl.num_programs(0) - 1)
    def _():
        place_rows(places, total, sent, 1 - core, ctx_axis)


def key_grad_kernel(ctx_axis, tokens, places, weights, score_grads, queries, grads, kept, total):
    step = pl.program_id(0)
    me = lax.axis_index("ctx")
    rank = grads.shape[1]
    half = total.shape[0]

    @pl.when(step == 0)
    def _():
        total[...] = jnp.zeros_like(total)

    first = places[me * tokens + step * RUN]
    visible_steps = ((first // RUN) * (RUN // 2)) // STEP + 1

    def run_of_queries(steps):
        seen = steps * STEP
        total[:seen, :] += dot_nn(score_grads[0, 0, :seen, :], queries[...])
        total[:seen, :rank] += dot_nn(weights[0, :seen, :], grads[...])

    for steps in range(1, half // STEP + 1):
        pl.when(visible_steps == steps)(functools.partial(run_of_queries, steps))

    @pl.when(step == pl.num_programs(0) - 1)
    def _():
        place_rows(places, total, kept, me & 1, ctx_axis)


def query_grad_kernel(heads, tokens, places, score_grads, keys, cosine, sine, d_latent, d_rope):
    step = pl.program_id(0)
    me = lax.axis_index("ctx")
    rows, rank = d_latent.shape
    rope = d_rope.shape[1]
    span = TILE // heads
    first = places[me * tokens + step * RUN]
    visible_steps = ((first // RUN) * (RUN // 2)) // STEP + 1

    def run_of_queries(steps):
        seen = steps * STEP
        for tile in range(rows // TILE):
            here = slice(tile * TILE, (tile + 1) * TILE)
            own = slice(tile * span, (tile + 1) * span)
            value = dot_tn(score_grads[0, 0, :seen, here], keys[0, :seen, :])
            value += dot_tn(score_grads[0, 1, :seen, here], keys[1, :seen, :])
            d_latent[here, :] = value[:, :rank].astype(BF16)
            turned = value[:, rank : rank + rope]
            spread = lambda table: jnp.broadcast_to(table[own, :][:, None, :], (span, heads, rope)).reshape(TILE, rope)
            d_rope[here, :] = (turned * spread(cosine) - half_turn(turned) * spread(sine)).astype(BF16)

    for steps in range(1, keys.shape[1] // STEP + 1):
        pl.when(visible_steps == steps)(functools.partial(run_of_queries, steps))


def pair(values, distance, axis):
    count = lax.axis_size(axis)
    return lax.ppermute(values, axis, [(i, i ^ distance) for i in range(count)])


def body(q_latent, q_rope, latent, rope_key, positions, d_out, w_uv):
    tokens, heads, rank = q_latent.shape
    rope = rope_key.shape[1]
    value_width = d_out.shape[2]
    sequence = positions.shape[0]
    head_axis, ctx_axis = lax.axis_size("head"), lax.axis_size("ctx")
    out_rows = sequence // (head_axis * ctx_axis)
    half = sequence // 2
    width = rank + rope
    padded = -(-width // 128) * 128
    rows = tokens * heads
    runs = tokens // RUN
    run_rows = RUN * heads
    scaling = (NOPE + rope) ** -0.5
    inverse = ROPE_BASE ** (-(np.arange(rope // 2, dtype=np.float64) / (rope // 2)))
    inverse = jnp.asarray(np.concatenate([inverse, inverse])[None, :].astype(np.float32))

    def shape(*dims, dtype=BF16):
        return jax.ShapeDtypeStruct(dims, dtype)

    def cost(flops, nbytes, more=0):
        return pl.CostEstimate(flops=flops, bytes_accessed=nbytes, transcendentals=more)

    own_keys, cosine, sine, out_cosine, out_sine = pl.pallas_call(
        functools.partial(key_kernel, head_axis, ctx_axis),
        out_shape=(
            shape(tokens, width),
            shape(tokens, rope, dtype=F32),
            shape(tokens, rope, dtype=F32),
            shape(out_rows, rope, dtype=F32),
            shape(out_rows, rope, dtype=F32),
        ),
        in_specs=[smem(), vmem(), vmem(), vmem()],
        out_specs=(vmem(),) * 5,
        compiler_params=params(16),
        name="own_keys",
    )(positions, latent, rope_key, inverse)

    blocks = [own_keys] + [None] * (ctx_axis - 1)
    for chip in range(1, ctx_axis // 2):
        blocks[2 * chip] = pair(own_keys, 2 * chip, "ctx")
    for chip in range(ctx_axis // 2):
        blocks[2 * chip + 1] = pair(blocks[2 * chip], 1, "ctx")

    query_rows, grad_rows = pl.pallas_call(
        functools.partial(query_kernel, heads),
        out_shape=(shape(rows, padded), shape(rows, rank)),
        in_specs=[vmem()] * 6,
        out_specs=(vmem(),) * 2,
        scratch_shapes=[
            pltpu.VMEM((heads, tokens, value_width), BF16),
            pltpu.VMEM((heads, tokens, rank), BF16),
        ],
        compiler_params=params(32),
        cost_estimate=cost(2 * rows * rank * value_width, 10 * MIB),
        name="query_rows",
    )(
        q_latent.reshape(rows, rank),
        q_rope.reshape(rows, rope),
        cosine,
        sine,
        d_out.reshape(rows, value_width),
        w_uv,
    )

    slots = (ctx_axis // 2, head_axis, out_rows, width)
    run_block = lambda columns: pl.BlockSpec((run_rows, columns), lambda i: (i, 0))
    sent, keys, weights_kept, score_grads = pl.pallas_call(
        functools.partial(front_kernel, ctx_axis, heads, tokens, out_rows, scaling),
        grid=(runs,),
        out_shape=(
            shape(*slots),
            shape(2, half, padded),
            shape(runs, half, run_rows),
            shape(runs, 2, half, run_rows),
        ),
        in_specs=[smem()] + [whole((tokens, width))] * ctx_axis + [run_block(padded), run_block(rank)],
        out_specs=(
            whole(slots),
            whole((2, half, padded)),
            pl.BlockSpec((1, half, run_rows), lambda i: (i, 0, 0)),
            pl.BlockSpec((1, 2, half, run_rows), lambda i: (i, 0, 0, 0)),
        ),
        scratch_shapes=[
            pltpu.VMEM((half, run_rows), BF16),
            pltpu.VMEM((half, padded), F32),
            pltpu.VMEM((2, sequence, TILE), F32),
            pltpu.VMEM((2, sequence, TILE), F32),
        ],
        compiler_params=params(56),
        cost_estimate=cost(7 * rows * sequence * width, 20 * MIB),
        name="front",
    )(positions, *blocks, query_rows, grad_rows)

    received = pair(sent, 1, "ctx")

    kept = pl.pallas_call(
        functools.partial(key_grad_kernel, ctx_axis, tokens),
        grid=(runs,),
        out_shape=shape(*slots),
        in_specs=[
            smem(),
            pl.BlockSpec((1, half, run_rows), lambda i: (i, 0, 0)),
            pl.BlockSpec((1, 1, half, run_rows), lambda i: (i, 1, 0, 0)),
            run_block(padded),
            run_block(rank),
        ],
        out_specs=whole(slots),
        scratch_shapes=[pltpu.VMEM((half, padded), F32)],
        compiler_params=params(40),
        cost_estimate=cost(2 * rows * sequence * width, 10 * MIB),
        name="key_grad",
    )(positions, weights_kept, score_grads, query_rows, grad_rows)

    pair_sum = kept.astype(F32) + received.astype(F32)
    pair_low = pair_sum.astype(BF16)
    plane_sum = pair_sum[0]
    for chip in range(1, ctx_axis // 2):
        plane_sum = plane_sum + pair(pair_low[chip], 2 * chip, "ctx").astype(F32)

    d_q_latent, d_q_rope = pl.pallas_call(
        functools.partial(query_grad_kernel, heads, tokens),
        grid=(runs,),
        out_shape=(shape(rows, rank), shape(rows, rope)),
        in_specs=[
            smem(),
            pl.BlockSpec((1, 2, half, run_rows), lambda i: (i, 0, 0, 0)),
            whole((2, half, padded)),
            pl.BlockSpec((RUN, rope), lambda i: (i, 0)),
            pl.BlockSpec((RUN, rope), lambda i: (i, 0)),
        ],
        out_specs=(run_block(rank), run_block(rope)),
        compiler_params=params(40),
        cost_estimate=cost(2 * rows * sequence * width, 10 * MIB),
        name="query_grad",
    )(positions, score_grads, keys, cosine, sine)

    plane_low = plane_sum.astype(BF16)
    mine = lax.axis_index("head")
    own = lax.dynamic_index_in_dim(plane_sum, mine, 0, keepdims=False)
    for far in range(1, head_axis):
        part = lax.dynamic_index_in_dim(plane_low, mine ^ far, 0, keepdims=False)
        own = own + pair(part, far, "head").astype(F32)

    turned = own[:, rank:]
    d_rope_key = turned * out_cosine - half_turn(turned) * out_sine
    return (
        d_q_latent.reshape(tokens, heads, rank),
        d_q_rope.reshape(tokens, heads, rope),
        own[:, :rank],
        d_rope_key,
    )


def solution(mesh):
    placed = (
        P("ctx", "head", None),
        P("ctx", "head", None),
        P("ctx", None),
        P("ctx", None),
        P(),
        P("ctx", "head", None),
        P("head", None, None),
    )
    return jax.shard_map(
        body,
        mesh=mesh,
        in_specs=placed,
        out_specs=(
            P("ctx", "head", None),
            P("ctx", "head", None),
            P(("head", "ctx"), None),
            P(("head", "ctx"), None),
        ),
        check_vma=False,
    )
```

```python
import functools
import math

import jax
import jax.numpy as jnp
import numpy as np
from jax import lax
from jax.experimental import pallas as pl
from jax.experimental.pallas import tpu as pltpu
from jax.sharding import PartitionSpec as P

NOPE = 128
RUN = 64
TILE = 256
STEP = 128
ROPE_BASE = 10000.0
NEGATIVE = -1e30
MIB = 1 << 20
BF16 = jnp.bfloat16
F32 = jnp.float32


def dot_nn(left, right):
    return lax.dot_general(left, right, (((1,), (0,)), ((), ())), preferred_element_type=F32)


def dot_nt(left, right):
    return lax.dot_general(left, right, (((1,), (1,)), ((), ())), preferred_element_type=F32)


def dot_tn(left, right):
    return lax.dot_general(left, right, (((0,), (0,)), ((), ())), preferred_element_type=F32)


def half_turn(values):
    middle = values.shape[0] // 2
    return jnp.concatenate([-values[middle:], values[:middle]], 0)


def half_turn_last(values):
    middle = values.shape[-1] // 2
    return jnp.concatenate([-values[..., middle:], values[..., :middle]], -1)


def vmem():
    return pl.BlockSpec(memory_space=pltpu.VMEM)


def smem():
    return pl.BlockSpec(memory_space=pltpu.SMEM)


def whole(shape):
    return pl.BlockSpec(shape, lambda *_: (0,) * len(shape))


def params(mib):
    return pltpu.CompilerParams(vmem_limit_bytes=mib * MIB)


def key_kernel(head_axis, ctx_axis, places, latent, rope, inverse, keys, cosine, sine, own_cosine, own_sine, out_cosine, out_sine):
    me = lax.axis_index("ctx")
    tokens, rank = latent.shape
    width = rope.shape[0]
    lanes = lax.broadcasted_iota(jnp.int32, (width, tokens), 1)
    count = lanes
    for run in range(tokens // RUN):
        first = places[me * tokens + run * RUN] - run * RUN
        count = jnp.where((lanes >> (RUN.bit_length() - 1)) == run, lanes + first, count)
    angles = count.astype(F32) * inverse[...]
    cosine[...] = jnp.cos(angles)
    sine[...] = jnp.sin(angles)
    own_cosine[...] = cosine[...].T
    own_sine[...] = sine[...].T
    values = rope[...].astype(F32)
    turned = values * cosine[...] + half_turn(values) * sine[...]
    keys[:, :rank] = latent[...]
    keys[:, rank:] = turned.T.astype(BF16)
    out_rows = out_cosine.shape[0]
    block = lax.axis_index("head") * ctx_axis + me
    first = places[block * out_rows]
    count = lax.broadcasted_iota(jnp.int32, (width, tokens), 1) + first
    angles = count.astype(F32) * inverse[...]
    out_cosine[...] = jnp.cos(angles).T[:out_rows, :]
    out_sine[...] = jnp.sin(angles).T[:out_rows, :]


def rows_to_heads(heads):
    span = TILE // heads
    shift_span, shift_heads = span.bit_length() - 1, heads.bit_length() - 1
    by_row = lax.broadcasted_iota(jnp.int32, (TILE, TILE), 0)
    by_column = lax.broadcasted_iota(jnp.int32, (TILE, TILE), 1)
    same = ((by_row >> shift_span) == (by_column & (heads - 1))) & (
        (by_row & (span - 1)) == (by_column >> shift_heads)
    )
    return jnp.where(same, 1.0, 0.0).astype(BF16)


def query_kernel(heads, q_latent, q_rope, cosine, sine, d_out, w_uv, queries, grads, by_head, grad_heads):
    rows, rank = q_latent.shape
    rope = q_rope.shape[1]
    span = TILE // heads
    to_heads = rows_to_heads(heads)
    tiles = rows // TILE
    queries[:, :rank] = q_latent[...]
    queries[:, rank + rope :] = jnp.zeros((rows, queries.shape[1] - rank - rope), BF16)
    for tile in range(tiles):
        here = slice(tile * TILE, (tile + 1) * TILE)
        own = slice(tile * span, (tile + 1) * span)
        by_head[:, own, :] = dot_nn(to_heads, d_out[here, :]).astype(BF16).reshape(heads, span, d_out.shape[1])
    for head in range(heads):
        grad_heads[head, :, :rank] = dot_nt(by_head[head], w_uv[head]).astype(BF16)
        values = q_rope[head].astype(F32)
        turned = values * cosine[...] + half_turn(values) * sine[...]
        grad_heads[head, :, rank:] = turned.T.astype(BF16)
    for tile in range(tiles):
        here = slice(tile * TILE, (tile + 1) * TILE)
        own = slice(tile * span, (tile + 1) * span)
        block = grad_heads[:, own, :].reshape(TILE, rank + rope)
        block = dot_tn(to_heads, block).astype(BF16)
        grads[here, :] = block[:, :rank]
        queries[here, rank : rank + rope] = block[:, rank:]


def place_rows(places, total, out, core, ctx_axis):
    out_rows, width = out.shape[2], out.shape[3]
    chip = lax.axis_index("ctx") >> 1
    half_run = RUN // 2
    for run in range(places.shape[0] // RUN):
        rank_of_run = places[run * RUN] // RUN
        for piece in range(half_run // out_rows):
            block = run * (RUN // out_rows) + 2 * piece
            source = pl.ds(pl.multiple_of(rank_of_run * half_run + piece * out_rows, out_rows), out_rows)
            slot = ((block % ctx_axis) >> 1) ^ chip
            out[slot, block // ctx_axis] = total[source, :width].astype(out.dtype)


def front_kernel(ctx_axis, heads, tokens, out_rows, scaling, places, *refs):
    blocks = refs[:ctx_axis]
    queries, grads, sent, keys, weights_kept, score_grads, weights_sent, total, scores, upstream = refs[ctx_axis:]
    step = pl.program_id(0)
    me = lax.axis_index("ctx")
    core = me & 1
    half_run = RUN // 2
    half = keys.shape[1]
    rank = grads.shape[1]
    width = blocks[0].shape[1]
    rows = queries.shape[0]

    @pl.when(step == 0)
    def _():
        total[...] = jnp.zeros_like(total)
        keys[:, :, width:] = jnp.zeros((2, half, keys.shape[2] - width), BF16)
        for far in range(ctx_axis):
            for run in range(tokens // RUN):
                rank_of_run = places[(me ^ far) * tokens + run * RUN] // RUN
                for sub in range(RUN // out_rows):
                    group = (core ^ (sub & 1)) ^ 1
                    start = pl.multiple_of(rank_of_run * half_run + (sub // 2) * out_rows, out_rows)
                    piece = blocks[far][run * RUN + sub * out_rows : run * RUN + (sub + 1) * out_rows, :]
                    keys[group, pl.ds(start, out_rows), :width] = piece

    first = places[me * tokens + step * RUN]
    visible_steps = ((first // RUN) * half_run) // STEP + 1

    def run_of_queries(steps):
        seen = steps * STEP
        for tile in range(rows // TILE):
            here = slice(tile * TILE, (tile + 1) * TILE)
            score, up = scores.at[tile % 2], upstream.at[tile % 2]
            tile_queries = queries[here, :]
            tile_grads = grads[here, :]
            lanes = lax.broadcasted_iota(jnp.int32, (1, TILE), 1)
            query_places = first + ((lanes + tile * TILE) >> (heads.bit_length() - 1))
            peak = jnp.full((8, TILE), NEGATIVE, F32)
            for group in range(2):
                for part in range(steps):
                    at = slice(group * seen + part * STEP, group * seen + (part + 1) * STEP)
                    value = dot_nt(keys[group, part * STEP : (part + 1) * STEP, :], tile_queries)
                    if part == steps - 1:
                        index = lax.broadcasted_iota(jnp.int32, (STEP, 1), 0) + part * STEP
                        bit = core ^ (1 - group)
                        key_places = index + (index & ~(out_rows - 1)) + bit * out_rows
                        value = jnp.where(key_places <= query_places, value, NEGATIVE)
                    score[at, :] = value
                    peak = jnp.maximum(peak, jnp.max(value.reshape(STEP // 8, 8, TILE), axis=0))
                    up[at, :] = dot_nt(keys[group, part * STEP : (part + 1) * STEP, :rank], tile_grads)
            factor = scaling * math.log2(math.e)
            peak = jnp.max(peak, axis=0, keepdims=True) * factor
            sums = jnp.zeros((8, TILE), F32)
            mixed = jnp.zeros((8, TILE), F32)
            piece = 64
            for part in range(2 * seen // piece):
                at = slice(part * piece, (part + 1) * piece)
                value = jnp.exp2(score[at, :] * factor - peak)
                score[at, :] = value
                sums += jnp.sum(value.reshape(piece // 8, 8, TILE), axis=0)
                mixed += jnp.sum((value * up[at, :]).reshape(piece // 8, 8, TILE), axis=0)
            inverse = 1.0 / jnp.sum(sums, axis=0, keepdims=True)
            diagonal = jnp.sum(mixed, axis=0, keepdims=True) * inverse
            scaled = inverse * scaling
            for part in range(2 * seen // piece):
                at = slice(part * piece, (part + 1) * piece)
                group, row = (part * piece) // seen, (part * piece) % seen
                to = slice(row, row + piece)
                value = score[at, :]
                weight = (value * inverse).astype(BF16)
                if group == 0:
                    weights_sent[to, here] = weight
                else:
                    weights_kept[0, to, here] = weight
                grad = (value * scaled) * (up[at, :] - diagonal)
                score_grads[0, group, to, here] = grad.astype(BF16)
        total[:seen, :] += dot_nn(score_grads[0, 0, :seen, :], queries[...])
        total[:seen, :rank] += dot_nn(weights_sent[:seen, :], grads[...])

    for steps in range(1, half // STEP + 1):
        pl.when(visible_steps == steps)(functools.partial(run_of_queries, steps))

    @pl.when(step == pl.num_programs(0) - 1)
    def _():
        place_rows(places, total, sent, 1 - core, ctx_axis)


def key_grad_kernel(ctx_axis, tokens, places, weights, score_grads, queries, grads, kept, total):
    step = pl.program_id(0)
    me = lax.axis_index("ctx")
    rank = grads.shape[1]
    half = total.shape[0]

    @pl.when(step == 0)
    def _():
        total[...] = jnp.zeros_like(total)

    first = places[me * tokens + step * RUN]
    visible_steps = ((first // RUN) * (RUN // 2)) // STEP + 1

    def run_of_queries(steps):
        seen = steps * STEP
        total[:seen, :] += dot_nn(score_grads[0, 0, :seen, :], queries[...])
        total[:seen, :rank] += dot_nn(weights[0, :seen, :], grads[...])

    for steps in range(1, half // STEP + 1):
        pl.when(visible_steps == steps)(functools.partial(run_of_queries, steps))

    @pl.when(step == pl.num_programs(0) - 1)
    def _():
        place_rows(places, total, kept, me & 1, ctx_axis)


def query_grad_kernel(heads, tokens, places, score_grads, keys, cosine, sine, d_latent, d_rope, by_head):
    step = pl.program_id(0)
    me = lax.axis_index("ctx")
    rows, rank = d_latent.shape
    rope = d_rope.shape[1]
    span = TILE // heads
    to_heads = rows_to_heads(heads)
    first = places[me * tokens + step * RUN]
    visible_steps = ((first // RUN) * (RUN // 2)) // STEP + 1

    def run_of_queries(steps):
        seen = steps * STEP
        for tile in range(rows // TILE):
            here = slice(tile * TILE, (tile + 1) * TILE)
            own = slice(tile * span, (tile + 1) * span)
            value = dot_tn(score_grads[0, 0, :seen, here], keys[0, :seen, :])
            value += dot_tn(score_grads[0, 1, :seen, here], keys[1, :seen, :])
            d_latent[here, :] = value[:, :rank].astype(BF16)
            turned = value[:, rank : rank + rope]
            spread = lambda table: jnp.broadcast_to(table[own, :][:, None, :], (span, heads, rope)).reshape(TILE, rope)
            turned = (turned * spread(cosine) - half_turn_last(turned) * spread(sine)).astype(BF16)
            turned = dot_nn(to_heads, turned).reshape(heads, span, rope)
            by_head[:, pl.ds(pl.multiple_of(step * RUN + tile * span, span), span), :] = turned

    for steps in range(1, keys.shape[1] // STEP + 1):
        pl.when(visible_steps == steps)(functools.partial(run_of_queries, steps))

    @pl.when(step == pl.num_programs(0) - 1)
    def _():
        for head in range(heads):
            d_rope[head] = by_head[head].T.astype(BF16)


def pair_sum_kernel(kept, received, own, *others):
    own[...] = kept[0].astype(F32) + received[0].astype(F32)
    for chip, out in enumerate(others):
        out[...] = (kept[chip + 1].astype(F32) + received[chip + 1].astype(F32)).astype(BF16)


def plane_sum_kernel(own, *refs):
    head_axis = own.shape[0]
    received, kept, others = refs[: -head_axis], refs[-head_axis], refs[1 - head_axis :]
    mine = lax.axis_index("head")
    for far in range(head_axis):
        value = own[mine ^ far]
        for part in received:
            value += part[mine ^ far].astype(F32)
        if far == 0:
            kept[...] = value
        else:
            others[far - 1][...] = value.astype(BF16)


def head_sum_kernel(own, *refs):
    received, cosine, sine, d_latent, d_rope = refs[:-4], *refs[-4:]
    rank = d_latent.shape[1]
    value = own[...]
    for part in received:
        value += part[...].astype(F32)
    d_latent[...] = value[:, :rank]
    turned = value[:, rank:]
    d_rope[...] = turned * cosine[...] - half_turn_last(turned) * sine[...]


def pair(values, distance, axis):
    count = lax.axis_size(axis)
    return lax.ppermute(values, axis, [(i, i ^ distance) for i in range(count)])


def body(q_latent, q_rope, latent, rope_key, positions, d_out, w_uv):
    tokens, heads, rank = q_latent.shape
    rope = rope_key.shape[1]
    value_width = d_out.shape[2]
    sequence = positions.shape[0]
    head_axis, ctx_axis = lax.axis_size("head"), lax.axis_size("ctx")
    out_rows = sequence // (head_axis * ctx_axis)
    half = sequence // 2
    width = rank + rope
    padded = -(-width // 128) * 128
    rows = tokens * heads
    runs = tokens // RUN
    run_rows = RUN * heads
    scaling = (NOPE + rope) ** -0.5
    inverse = ROPE_BASE ** (-(np.arange(rope // 2, dtype=np.float64) / (rope // 2)))
    inverse = jnp.asarray(np.tile(np.concatenate([inverse, inverse])[:, None], (1, tokens)).astype(np.float32))

    def shape(*dims, dtype=BF16):
        return jax.ShapeDtypeStruct(dims, dtype)

    def cost(flops, nbytes, more=0):
        return pl.CostEstimate(flops=flops, bytes_accessed=nbytes, transcendentals=more)

    own_keys, cosine, sine, own_cosine, own_sine, out_cosine, out_sine = pl.pallas_call(
        functools.partial(key_kernel, head_axis, ctx_axis),
        out_shape=(shape(tokens, width),)
        + (shape(rope, tokens, dtype=F32),) * 2
        + (shape(tokens, rope, dtype=F32),) * 2
        + (shape(out_rows, rope, dtype=F32),) * 2,
        in_specs=[smem(), vmem(), vmem(), vmem()],
        out_specs=(vmem(),) * 7,
        compiler_params=params(60),
        name="own_keys",
    )(positions, latent, rope_key.T, inverse)

    blocks = [own_keys] + [None] * (ctx_axis - 1)
    for chip in range(1, ctx_axis // 2):
        blocks[2 * chip] = pair(own_keys, 2 * chip, "ctx")

    query_rows, grad_rows = pl.pallas_call(
        functools.partial(query_kernel, heads),
        out_shape=(shape(rows, padded), shape(rows, rank)),
        in_specs=[vmem()] * 6,
        out_specs=(vmem(),) * 2,
        scratch_shapes=[
            pltpu.VMEM((heads, tokens, value_width), BF16),
            pltpu.VMEM((heads, tokens, width), BF16),
        ],
        compiler_params=params(24),
        cost_estimate=cost(2 * rows * rank * value_width, 10 * MIB),
        name="query_rows",
    )(
        q_latent.reshape(rows, rank),
        q_rope.transpose(1, 2, 0),
        cosine,
        sine,
        d_out.reshape(rows, value_width),
        w_uv,
    )

    blocks, query_rows, grad_rows = lax.optimization_barrier((blocks[::2], query_rows, grad_rows))
    blocks = [block for chip in blocks for block in (chip, pair(chip, 1, "ctx"))]

    slots = (ctx_axis // 2, head_axis, out_rows, width)
    run_block = lambda columns: pl.BlockSpec((run_rows, columns), lambda i: (i, 0))
    sent, keys, weights_kept, score_grads = pl.pallas_call(
        functools.partial(front_kernel, ctx_axis, heads, tokens, out_rows, scaling),
        grid=(runs,),
        out_shape=(
            shape(*slots),
            shape(2, half, padded),
            shape(runs, half, run_rows),
            shape(runs, 2, half, run_rows),
        ),
        in_specs=[smem()] + [whole((tokens, width))] * ctx_axis + [run_block(padded), run_block(rank)],
        out_specs=(
            whole(slots),
            whole((2, half, padded)),
            pl.BlockSpec((1, half, run_rows), lambda i: (i, 0, 0)),
            pl.BlockSpec((1, 2, half, run_rows), lambda i: (i, 0, 0, 0)),
        ),
        scratch_shapes=[
            pltpu.VMEM((half, run_rows), BF16),
            pltpu.VMEM((half, padded), F32),
            pltpu.VMEM((2, sequence, TILE), F32),
            pltpu.VMEM((2, sequence, TILE), F32),
        ],
        compiler_params=params(30),
        cost_estimate=cost(7 * rows * sequence * width, 20 * MIB),
        name="front",
    )(positions, *blocks, query_rows, grad_rows)

    received = pair(sent, 1, "ctx")

    kept = pl.pallas_call(
        functools.partial(key_grad_kernel, ctx_axis, tokens),
        grid=(runs,),
        out_shape=shape(*slots),
        in_specs=[
            smem(),
            pl.BlockSpec((1, half, run_rows), lambda i: (i, 0, 0)),
            pl.BlockSpec((1, 1, half, run_rows), lambda i: (i, 1, 0, 0)),
            run_block(padded),
            run_block(rank),
        ],
        out_specs=whole(slots),
        scratch_shapes=[pltpu.VMEM((half, padded), F32)],
        compiler_params=params(20),
        cost_estimate=cost(2 * rows * sequence * width, 10 * MIB),
        name="key_grad",
    )(positions, weights_kept, score_grads, query_rows, grad_rows)

    def small(kernel, outs, *operands):
        return pl.pallas_call(
            kernel,
            out_shape=outs,
            in_specs=[vmem()] * len(operands),
            out_specs=(vmem(),) * len(outs),
            compiler_params=params(4),
            name=kernel.__name__,
        )(*operands)

    low, high = shape(*slots[1:]), shape(*slots[1:], dtype=F32)
    own, *others = small(pair_sum_kernel, (high,) + (low,) * (slots[0] - 1), kept, received)
    others = [pair(part, 2 * (chip + 1), "ctx") for chip, part in enumerate(others)]

    d_q_latent, d_q_rope = pl.pallas_call(
        functools.partial(query_grad_kernel, heads, tokens),
        grid=(runs,),
        out_shape=(shape(rows, rank), shape(heads, rope, tokens)),
        in_specs=[
            smem(),
            pl.BlockSpec((1, 2, half, run_rows), lambda i: (i, 0, 0, 0)),
            whole((2, half, padded)),
            pl.BlockSpec((RUN, rope), lambda i: (i, 0)),
            pl.BlockSpec((RUN, rope), lambda i: (i, 0)),
        ],
        out_specs=(run_block(rank), whole((heads, rope, tokens))),
        scratch_shapes=[pltpu.VMEM((heads, tokens, rope), F32)],
        compiler_params=params(20),
        cost_estimate=cost(2 * rows * sequence * width, 10 * MIB),
        name="query_grad",
    )(positions, score_grads, keys, own_cosine, own_sine)

    others, d_q_latent, d_q_rope = lax.optimization_barrier((others, d_q_latent, d_q_rope))
    low, high = shape(*slots[2:]), shape(*slots[2:], dtype=F32)
    own, *others = small(plane_sum_kernel, (high,) + (low,) * (head_axis - 1), own, *others)
    others = [pair(part, far + 1, "head") for far, part in enumerate(others)]
    d_latent, d_rope_key = small(
        head_sum_kernel,
        (shape(out_rows, rank, dtype=F32), shape(out_rows, rope, dtype=F32)),
        own,
        *others,
        out_cosine,
        out_sine,
    )
    return (
        d_q_latent.reshape(tokens, heads, rank),
        d_q_rope.transpose(2, 0, 1),
        d_latent,
        d_rope_key,
    )


def solution(mesh):
    placed = (
        P("ctx", "head", None),
        P("ctx", "head", None),
        P("ctx", None),
        P("ctx", None),
        P(),
        P("ctx", "head", None),
        P("head", None, None),
    )
    return jax.shard_map(
        body,
        mesh=mesh,
        in_specs=placed,
        out_specs=(
            P("ctx", "head", None),
            P("ctx", "head", None),
            P(("head", "ctx"), None),
            P(("head", "ctx"), None),
        ),
        check_vma=False,
    )
```

```python
import functools
import math

import jax
import jax.numpy as jnp
import numpy as np
from jax import lax
from jax.experimental import pallas as pl
from jax.experimental.pallas import tpu as pltpu
from jax.sharding import PartitionSpec as P

NOPE = 128
RUN = 64
TILE = 256
PIECE = 64
WIDE = 512
STEP = 128
ROPE_BASE = 10000.0
NEGATIVE = -1e30
MIB = 1 << 20
BF16 = jnp.bfloat16
F32 = jnp.float32


def dot_nn(left, right):
    return lax.dot_general(left, right, (((1,), (0,)), ((), ())), preferred_element_type=F32)


def dot_nt(left, right):
    return lax.dot_general(left, right, (((1,), (1,)), ((), ())), preferred_element_type=F32)


def dot_tn(left, right):
    return lax.dot_general(left, right, (((0,), (0,)), ((), ())), preferred_element_type=F32)


def half_turn(values):
    middle = values.shape[0] // 2
    return jnp.concatenate([-values[middle:], values[:middle]], 0)


def half_turn_last(values):
    middle = values.shape[-1] // 2
    return jnp.concatenate([-values[..., middle:], values[..., :middle]], -1)


def vmem():
    return pl.BlockSpec(memory_space=pltpu.VMEM)


def smem():
    return pl.BlockSpec(memory_space=pltpu.SMEM)


def params(mib):
    return pltpu.CompilerParams(vmem_limit_bytes=mib * MIB)


def twice(values):
    return jnp.concatenate([values, values], 0)


def key_kernel(head_axis, ctx_axis, places, latent, rope, inverse, *refs):
    keys, tables, own_cosine, own_sine, out_cosine, out_sine = refs
    cosine, sine = tables.at[0], tables.at[1]
    me = lax.axis_index("ctx")
    tokens, rank = latent.shape
    lanes = lax.broadcasted_iota(jnp.int32, inverse.shape, 1)
    count = lanes
    for run in range(tokens // RUN):
        first = places[me * tokens + run * RUN] - run * RUN
        count = jnp.where((lanes >> (RUN.bit_length() - 1)) == run, lanes + first, count)
    angles = count.astype(F32) * inverse[...]
    cosine[...] = twice(jnp.cos(angles))
    sine[...] = twice(jnp.sin(angles))
    own_cosine[...] = cosine[...].T
    own_sine[...] = sine[...].T
    values = rope[...].astype(F32)
    turned = values * cosine[...] + half_turn(values) * sine[...]
    keys[:, :rank] = latent[...]
    keys[:, rank:] = turned.T.astype(BF16)
    out_rows = out_cosine.shape[0]
    first = places[(lax.axis_index("head") * ctx_axis + me) * out_rows]
    angles = (lanes + first).astype(F32) * inverse[...]
    out_cosine[...] = twice(jnp.cos(angles)).T[:out_rows, :]
    out_sine[...] = twice(jnp.sin(angles)).T[:out_rows, :]


def rows_to_heads(heads):
    span = TILE // heads
    shift_span, shift_heads = span.bit_length() - 1, heads.bit_length() - 1
    by_row = lax.broadcasted_iota(jnp.int32, (TILE, TILE), 0)
    by_column = lax.broadcasted_iota(jnp.int32, (TILE, TILE), 1)
    same = ((by_row >> shift_span) == (by_column & (heads - 1))) & (
        (by_row & (span - 1)) == (by_column >> shift_heads)
    )
    return jnp.where(same, 1.0, 0.0).astype(BF16)


def query_kernel(heads, q_latent, q_rope, d_out, w_uv, tables, queries, grads, by_head, grad_heads):
    cosine, sine = tables.at[0], tables.at[1]
    rows, rank = q_latent.shape
    rope = q_rope.shape[1]
    span = TILE // heads
    to_heads = rows_to_heads(heads)
    tiles = rows // TILE
    queries[:, :rank] = q_latent[...]
    queries[:, rank + rope :] = jnp.zeros((rows, queries.shape[1] - rank - rope), BF16)
    for tile in range(tiles):
        here = slice(tile * TILE, (tile + 1) * TILE)
        own = slice(tile * span, (tile + 1) * span)
        by_head[:, own, :] = dot_nn(to_heads, d_out[here, :]).astype(BF16).reshape(heads, span, d_out.shape[1])
    for head in range(heads):
        grad_heads[head, :, :rank] = dot_nt(by_head[head], w_uv[head]).astype(BF16)
        values = q_rope[head].astype(F32)
        turned = values * cosine[...] + half_turn(values) * sine[...]
        grad_heads[head, :, rank:] = turned.T.astype(BF16)
    for tile in range(tiles):
        here = slice(tile * TILE, (tile + 1) * TILE)
        own = slice(tile * span, (tile + 1) * span)
        block = grad_heads[:, own, :].reshape(TILE, rank + rope)
        block = dot_tn(to_heads, block).astype(BF16)
        grads[here, :] = block[:, :rank]
        queries[here, rank : rank + rope] = block[:, rank:]


def place_rows(places, total, out, core, ctx_axis):
    out_rows, width = out.shape[2], out.shape[3]
    chip = lax.axis_index("ctx") >> 1
    half_run = RUN // 2
    for run in range(places.shape[0] // RUN):
        rank_of_run = places[run * RUN] // RUN
        for piece in range(half_run // out_rows):
            block = run * (RUN // out_rows) + 2 * piece
            source = pl.ds(pl.multiple_of(rank_of_run * half_run + piece * out_rows, out_rows), out_rows)
            slot = ((block % ctx_axis) >> 1) ^ chip
            out[slot, block // ctx_axis] = total[source, :width].astype(out.dtype)


def front_kernel(ctx_axis, heads, tokens, out_rows, scaling, places, *refs):
    blocks = refs[:ctx_axis]
    all_queries, all_grads, sent, keys, all_weights, all_score_grads, weights_sent, total, scores, upstream = refs[ctx_axis:]
    me = lax.axis_index("ctx")
    core = me & 1
    half_run = RUN // 2
    half = keys.shape[1]
    rank = all_grads.shape[1]
    width = blocks[0].shape[1]
    rows = RUN * heads

    total[...] = jnp.zeros_like(total)
    keys[:, :, width:] = jnp.zeros((2, half, keys.shape[2] - width), BF16)
    for far in range(ctx_axis):
        for run in range(tokens // RUN):
            rank_of_run = places[(me ^ far) * tokens + run * RUN] // RUN
            for sub in range(RUN // out_rows):
                group = (core ^ (sub & 1)) ^ 1
                start = pl.multiple_of(rank_of_run * half_run + (sub // 2) * out_rows, out_rows)
                piece = blocks[far][run * RUN + sub * out_rows : run * RUN + (sub + 1) * out_rows, :]
                keys[group, pl.ds(start, out_rows), :width] = piece

    @pl.loop(0, tokens // RUN)
    def _(step):
        own = pl.ds(pl.multiple_of(step * rows, rows), rows)
        queries, grads = all_queries.at[own], all_grads.at[own]
        weights_kept, score_grads = all_weights.at[step], all_score_grads.at[step]
        first = places[me * tokens + step * RUN]
        visible_steps = ((first // RUN) * half_run) // STEP + 1

        def run_of_queries(steps):
            seen = steps * STEP
            both = lambda columns: keys[:, :seen, :columns].reshape(2 * seen, columns)

            def multiply(tile):
                here = slice(tile * TILE, (tile + 1) * TILE)
                scores[tile % 2, : 2 * seen, :] = dot_nt(both(queries.shape[1]), queries[here, :])
                upstream[tile % 2, : 2 * seen, :] = dot_nt(both(rank), grads[here, :])

            def weigh(tile):
                here = slice(tile * TILE, (tile + 1) * TILE)
                score, up = scores.at[tile % 2], upstream.at[tile % 2]
                lanes = lax.broadcasted_iota(jnp.int32, (1, TILE), 1)
                query_places = first + ((lanes + tile * TILE) >> (heads.bit_length() - 1))
                index = lax.broadcasted_iota(jnp.int32, (STEP, 1), 0) + (steps - 1) * STEP
                peak = jnp.full((8, TILE), NEGATIVE, F32)
                for group in range(2):
                    for part in range(steps):
                        at = slice(group * seen + part * STEP, group * seen + (part + 1) * STEP)
                        value = score[at, :]
                        if part == steps - 1:
                            bit = core ^ (1 - group)
                            key_places = index + (index & ~(out_rows - 1)) + bit * out_rows
                            value = jnp.where(key_places <= query_places, value, NEGATIVE)
                            score[at, :] = value
                        peak = jnp.maximum(peak, jnp.max(value.reshape(STEP // 8, 8, TILE), axis=0))
                factor = scaling * math.log2(math.e)
                peak = jnp.max(peak, axis=0, keepdims=True) * factor
                sums = jnp.zeros((8, TILE), F32)
                mixed = jnp.zeros((8, TILE), F32)
                for part in range(2 * seen // PIECE):
                    at = slice(part * PIECE, (part + 1) * PIECE)
                    value = jnp.exp2(score[at, :] * factor - peak)
                    score[at, :] = value
                    sums += jnp.sum(value.reshape(PIECE // 8, 8, TILE), axis=0)
                    mixed += jnp.sum((value * up[at, :]).reshape(PIECE // 8, 8, TILE), axis=0)
                inverse = 1.0 / jnp.sum(sums, axis=0, keepdims=True)
                diagonal = jnp.sum(mixed, axis=0, keepdims=True) * inverse
                scaled = inverse * scaling
                for part in range(2 * seen // PIECE):
                    at = slice(part * PIECE, (part + 1) * PIECE)
                    group, row = (part * PIECE) // seen, (part * PIECE) % seen
                    to = slice(row, row + PIECE)
                    value = score[at, :]
                    weight = (value * inverse).astype(BF16)
                    if group == 0:
                        weights_sent[to, here] = weight
                    else:
                        weights_kept[to, here] = weight
                    grad = (value * scaled) * (up[at, :] - diagonal)
                    score_grads[group, to, here] = grad.astype(BF16)

            tiles = rows // TILE
            for tile in range(tiles):
                multiply(tile)
                weigh(tile)
            total[:seen, :] += dot_nn(score_grads[0, :seen, :], queries[...])
            total[:seen, :rank] += dot_nn(weights_sent[:seen, :], grads[...])
        for steps in range(1, half // STEP + 1):
            pl.when(visible_steps == steps)(functools.partial(run_of_queries, steps))

    place_rows(places, total, sent, 1 - core, ctx_axis)


def key_grad_kernel(ctx_axis, heads, tokens, places, weights, score_grads, queries, grads, kept, total):
    me = lax.axis_index("ctx")
    rank = grads.shape[1]
    half = total.shape[0]
    rows = RUN * heads
    total[...] = jnp.zeros_like(total)

    @pl.loop(0, tokens // RUN)
    def _(step):
        own = pl.ds(pl.multiple_of(step * rows, rows), rows)
        first = places[me * tokens + step * RUN]
        visible_steps = ((first // RUN) * (RUN // 2)) // STEP + 1

        def run_of_queries(steps):
            seen = steps * STEP
            total[:seen, :] += dot_nn(score_grads[step, 1, :seen, :], queries[own, :])
            total[:seen, :rank] += dot_nn(weights[step, :seen, :], grads[own, :])

        for steps in range(1, half // STEP + 1):
            pl.when(visible_steps == steps)(functools.partial(run_of_queries, steps))

    place_rows(places, total, kept, me & 1, ctx_axis)


def query_grad_kernel(heads, tokens, places, score_grads, keys, cosine, sine, d_latent, d_rope, by_head):
    me = lax.axis_index("ctx")
    rank, rope = d_latent.shape[1], d_rope.shape[1]
    rows = RUN * heads
    span = TILE // heads
    to_heads = rows_to_heads(heads)

    @pl.loop(0, tokens // RUN)
    def _(step):
        first = places[me * tokens + step * RUN]
        visible_steps = ((first // RUN) * (RUN // 2)) // STEP + 1

        def run_of_queries(steps):
            seen = steps * STEP
            seen_keys = keys[:, :seen, :].reshape(2 * seen, keys.shape[2])
            for piece in range(rows // WIDE):
                here = slice(piece * WIDE, (piece + 1) * WIDE)
                value = dot_tn(score_grads[step, :, :seen, here].reshape(2 * seen, WIDE), seen_keys)
                at = pl.ds(pl.multiple_of(step * rows + piece * WIDE, WIDE), WIDE)
                d_latent[at, :] = value[:, :rank].astype(BF16)
                for tile in range(WIDE // TILE):
                    start = step * RUN + (piece * WIDE + tile * TILE) // heads
                    own = pl.ds(pl.multiple_of(start, span), span)
                    spread = lambda table: jnp.broadcast_to(table[own, :][:, None, :], (span, heads, rope)).reshape(TILE, rope)
                    turned = value[tile * TILE : (tile + 1) * TILE, rank : rank + rope]
                    turned = (turned * spread(cosine) - half_turn_last(turned) * spread(sine)).astype(BF16)
                    by_head[:, own, :] = dot_nn(to_heads, turned).reshape(heads, span, rope)

        for steps in range(1, keys.shape[1] // STEP + 1):
            pl.when(visible_steps == steps)(functools.partial(run_of_queries, steps))

    for head in range(heads):
        d_rope[head] = by_head[head].T.astype(BF16)


def pair_sum_kernel(kept, received, own, *others):
    own[...] = kept[0].astype(F32) + received[0].astype(F32)
    for chip, out in enumerate(others):
        out[...] = (kept[chip + 1].astype(F32) + received[chip + 1].astype(F32)).astype(BF16)


def plane_sum_kernel(own, *refs):
    head_axis = own.shape[0]
    received, kept, others = refs[: -head_axis], refs[-head_axis], refs[1 - head_axis :]
    mine = lax.axis_index("head")
    for far in range(head_axis):
        value = own[mine ^ far]
        for part in received:
            value += part[mine ^ far].astype(F32)
        if far == 0:
            kept[...] = value
        else:
            others[far - 1][...] = value.astype(BF16)


def head_sum_kernel(own, *refs):
    received, cosine, sine, d_latent, d_rope = refs[:-4], *refs[-4:]
    rank = d_latent.shape[1]
    value = own[...]
    for part in received:
        value += part[...].astype(F32)
    d_latent[...] = value[:, :rank]
    turned = value[:, rank:]
    d_rope[...] = turned * cosine[...] - half_turn_last(turned) * sine[...]


def pair(values, distance, axis):
    count = lax.axis_size(axis)
    return lax.ppermute(values, axis, [(i, i ^ distance) for i in range(count)])


def body(q_latent, q_rope, latent, rope_key, positions, d_out, w_uv):
    tokens, heads, rank = q_latent.shape
    rope = rope_key.shape[1]
    value_width = d_out.shape[2]
    sequence = positions.shape[0]
    head_axis, ctx_axis = lax.axis_size("head"), lax.axis_size("ctx")
    out_rows = sequence // (head_axis * ctx_axis)
    half = sequence // 2
    width = rank + rope
    padded = -(-width // 128) * 128
    rows = tokens * heads
    runs = tokens // RUN
    run_rows = RUN * heads
    scaling = (NOPE + rope) ** -0.5
    inverse = ROPE_BASE ** (-(np.arange(rope // 2, dtype=np.float64) / (rope // 2)))
    inverse = jnp.asarray(np.tile(inverse[:, None], (1, tokens)).astype(np.float32))

    def shape(*dims, dtype=BF16):
        return jax.ShapeDtypeStruct(dims, dtype)

    def cost(flops, nbytes, more=0):
        return pl.CostEstimate(flops=flops, bytes_accessed=nbytes, transcendentals=more)

    own_keys, tables, own_cosine, own_sine, out_cosine, out_sine = pl.pallas_call(
        functools.partial(key_kernel, head_axis, ctx_axis),
        out_shape=(shape(tokens, width),)
        + (shape(2, rope, tokens, dtype=F32),)
        + (shape(tokens, rope, dtype=F32),) * 2
        + (shape(out_rows, rope, dtype=F32),) * 2,
        in_specs=[smem(), vmem(), vmem(), vmem()],
        out_specs=(vmem(),) * 6,
        compiler_params=params(60),
        cost_estimate=cost(8 << 30, 32 * MIB),
        name="own_keys",
    )(positions, latent, rope_key.T, inverse)

    blocks = [own_keys] + [None] * (ctx_axis - 1)
    for chip in range(1, ctx_axis // 2):
        blocks[2 * chip] = pair(own_keys, 2 * chip, "ctx")

    query_rows, grad_rows = pl.pallas_call(
        functools.partial(query_kernel, heads),
        out_shape=(shape(rows, padded), shape(rows, rank)),
        in_specs=[vmem()] * 5,
        out_specs=(vmem(),) * 2,
        scratch_shapes=[
            pltpu.VMEM((heads, tokens, value_width), BF16),
            pltpu.VMEM((heads, tokens, width), BF16),
        ],
        compiler_params=params(24),
        cost_estimate=cost(2 * rows * rank * value_width, 10 * MIB),
        name="query_rows",
    )(
        q_latent.reshape(rows, rank),
        q_rope.transpose(1, 2, 0),
        d_out.reshape(rows, value_width),
        w_uv,
        tables,
    )

    blocks, query_rows, grad_rows = lax.optimization_barrier((blocks[::2], query_rows, grad_rows))
    blocks = [block for chip in blocks for block in (chip, pair(chip, 1, "ctx"))]

    slots = (ctx_axis // 2, head_axis, out_rows, width)
    sent, keys, weights_kept, score_grads = pl.pallas_call(
        functools.partial(front_kernel, ctx_axis, heads, tokens, out_rows, scaling),
        out_shape=(
            shape(*slots),
            shape(2, half, padded),
            shape(runs, half, run_rows),
            shape(runs, 2, half, run_rows),
        ),
        in_specs=[smem()] + [vmem()] * (ctx_axis + 2),
        out_specs=(vmem(),) * 4,
        scratch_shapes=[
            pltpu.VMEM((half, run_rows), BF16),
            pltpu.VMEM((half, padded), F32),
            pltpu.VMEM((2, sequence, TILE), F32),
            pltpu.VMEM((2, sequence, TILE), F32),
        ],
        compiler_params=params(30),
        cost_estimate=cost(7 * rows * sequence * width, 20 * MIB),
        name="front",
    )(positions, *blocks, query_rows, grad_rows)

    received = pair(sent, 1, "ctx")

    kept = pl.pallas_call(
        functools.partial(key_grad_kernel, ctx_axis, heads, tokens),
        out_shape=shape(*slots),
        in_specs=[smem()] + [vmem()] * 4,
        out_specs=vmem(),
        scratch_shapes=[pltpu.VMEM((half, padded), F32)],
        compiler_params=params(20),
        cost_estimate=cost(2 * rows * sequence * width, 10 * MIB),
        name="key_grad",
    )(positions, weights_kept, score_grads, query_rows, grad_rows)

    def small(kernel, outs, *operands):
        return pl.pallas_call(
            kernel,
            out_shape=outs,
            in_specs=[vmem()] * len(operands),
            out_specs=(vmem(),) * len(outs),
            compiler_params=params(4),
            name=kernel.__name__,
        )(*operands)

    low, high = shape(*slots[1:]), shape(*slots[1:], dtype=F32)
    own, *others = small(pair_sum_kernel, (high,) + (low,) * (slots[0] - 1), kept, received)
    others = [pair(part, 2 * (chip + 1), "ctx") for chip, part in enumerate(others)]

    d_q_latent, d_q_rope = pl.pallas_call(
        functools.partial(query_grad_kernel, heads, tokens),
        out_shape=(shape(rows, rank), shape(heads, rope, tokens)),
        in_specs=[smem()] + [vmem()] * 4,
        out_specs=(vmem(),) * 2,
        scratch_shapes=[pltpu.VMEM((heads, tokens, rope), F32)],
        compiler_params=params(20),
        cost_estimate=cost(2 * rows * sequence * width, 10 * MIB),
        name="query_grad",
    )(positions, score_grads, keys, own_cosine, own_sine)

    others, d_q_latent, d_q_rope = lax.optimization_barrier((others, d_q_latent, d_q_rope))
    low, high = shape(*slots[2:]), shape(*slots[2:], dtype=F32)
    own, *others = small(plane_sum_kernel, (high,) + (low,) * (head_axis - 1), own, *others)
    others = [pair(part, far + 1, "head") for far, part in enumerate(others)]
    d_latent, d_rope_key = small(
        head_sum_kernel,
        (shape(out_rows, rank, dtype=F32), shape(out_rows, rope, dtype=F32)),
        own,
        *others,
        out_cosine,
        out_sine,
    )
    return (
        d_q_latent.reshape(tokens, heads, rank),
        d_q_rope.transpose(2, 0, 1),
        d_latent,
        d_rope_key,
    )


def solution(mesh):
    placed = (
        P("ctx", "head", None),
        P("ctx", "head", None),
        P("ctx", None),
        P("ctx", None),
        P(),
        P("ctx", "head", None),
        P("head", None, None),
    )
    return jax.shard_map(
        body,
        mesh=mesh,
        in_specs=placed,
        out_specs=(
            P("ctx", "head", None),
            P("ctx", "head", None),
            P(("head", "ctx"), None),
            P(("head", "ctx"), None),
        ),
        check_vma=False,
    )
```

```python
import functools
import math

import jax
import jax.numpy as jnp
import numpy as np
from jax import lax
from jax.experimental import pallas as pl
from jax.experimental.pallas import tpu as pltpu
from jax.sharding import PartitionSpec as P

NOPE = 128
RUN = 64
TILE = 256
PIECE = 64
WIDE = 512
STEP = 128
ROPE_BASE = 10000.0
NEGATIVE = -1e30
MIB = 1 << 20
BF16 = jnp.bfloat16
F32 = jnp.float32


def dot_nn(left, right):
    return lax.dot_general(left, right, (((1,), (0,)), ((), ())), preferred_element_type=F32)


def dot_nt(left, right):
    return lax.dot_general(left, right, (((1,), (1,)), ((), ())), preferred_element_type=F32)


def dot_tn(left, right):
    return lax.dot_general(left, right, (((0,), (0,)), ((), ())), preferred_element_type=F32)


def half_turn(values):
    middle = values.shape[0] // 2
    return jnp.concatenate([-values[middle:], values[:middle]], 0)


def half_turn_last(values):
    middle = values.shape[-1] // 2
    return jnp.concatenate([-values[..., middle:], values[..., :middle]], -1)


def vmem():
    return pl.BlockSpec(memory_space=pltpu.VMEM)


def smem():
    return pl.BlockSpec(memory_space=pltpu.SMEM)


def params(mib):
    return pltpu.CompilerParams(vmem_limit_bytes=mib * MIB)


def twice(values):
    return jnp.concatenate([values, values], 0)


def key_kernel(head_axis, ctx_axis, out_rows, places, latent, rope, inverse, keys, tables):
    me = lax.axis_index("ctx")
    tokens, rank = latent.shape
    lanes = lax.broadcasted_iota(jnp.int32, inverse.shape, 1)
    count = lanes
    for run in range(tokens // RUN):
        first = places[me * tokens + run * RUN] - run * RUN
        count = jnp.where((lanes >> (RUN.bit_length() - 1)) == run, lanes + first, count)
    angles = count.astype(F32) * inverse[...]
    cosine, sine = jnp.cos(angles), jnp.sin(angles)
    values = rope[...].astype(F32)
    turned = values * twice(cosine) + half_turn(values) * twice(sine)
    keys[:, :rank] = latent[...]
    keys[:, rank:] = turned.T.astype(BF16)
    first = places[(lax.axis_index("head") * ctx_axis + me) * out_rows]
    tables[0] = cosine
    tables[1] = sine
    tables[2] = (lanes + first).astype(F32) * inverse[...]


def rows_to_heads(heads):
    span = TILE // heads
    shift_span, shift_heads = span.bit_length() - 1, heads.bit_length() - 1
    by_row = lax.broadcasted_iota(jnp.int32, (TILE, TILE), 0)
    by_column = lax.broadcasted_iota(jnp.int32, (TILE, TILE), 1)
    same = ((by_row >> shift_span) == (by_column & (heads - 1))) & (
        (by_row & (span - 1)) == (by_column >> shift_heads)
    )
    return jnp.where(same, 1.0, 0.0).astype(BF16)


def query_kernel(heads, q_latent, q_rope, d_out, w_uv, tables, *refs):
    queries, grads, own_cosine, own_sine, out_cosine, out_sine, by_head, grad_heads = refs
    cosine, sine = twice(tables[0]), twice(tables[1])
    own_cosine[...] = cosine.T
    own_sine[...] = sine.T
    out_cosine[...] = twice(jnp.cos(tables[2])).T[: out_cosine.shape[0], :]
    out_sine[...] = twice(jnp.sin(tables[2])).T[: out_sine.shape[0], :]
    rows, rank = q_latent.shape
    rope = q_rope.shape[1]
    span = TILE // heads
    to_heads = rows_to_heads(heads)
    tiles = rows // TILE
    queries[:, :rank] = q_latent[...]
    queries[:, rank + rope :] = jnp.zeros((rows, queries.shape[1] - rank - rope), BF16)
    for tile in range(tiles):
        here = slice(tile * TILE, (tile + 1) * TILE)
        own = slice(tile * span, (tile + 1) * span)
        by_head[:, own, :] = dot_nn(to_heads, d_out[here, :]).astype(BF16).reshape(heads, span, d_out.shape[1])
    for head in range(heads):
        grad_heads[head, :, :rank] = dot_nt(by_head[head], w_uv[head]).astype(BF16)
        values = q_rope[head].astype(F32)
        turned = values * cosine + half_turn(values) * sine
        grad_heads[head, :, rank:] = turned.T.astype(BF16)
    for tile in range(tiles):
        here = slice(tile * TILE, (tile + 1) * TILE)
        own = slice(tile * span, (tile + 1) * span)
        block = grad_heads[:, own, :].reshape(TILE, rank + rope)
        block = dot_tn(to_heads, block).astype(BF16)
        grads[here, :] = block[:, :rank]
        queries[here, rank : rank + rope] = block[:, rank:]


def place_rows(places, total, out, core, ctx_axis):
    out_rows, width = out.shape[2], out.shape[3]
    chip = lax.axis_index("ctx") >> 1
    half_run = RUN // 2
    for run in range(places.shape[0] // RUN):
        rank_of_run = places[run * RUN] // RUN
        for piece in range(half_run // out_rows):
            block = run * (RUN // out_rows) + 2 * piece
            source = pl.ds(pl.multiple_of(rank_of_run * half_run + piece * out_rows, out_rows), out_rows)
            slot = ((block % ctx_axis) >> 1) ^ chip
            out[slot, block // ctx_axis] = total[source, :width].astype(out.dtype)


def front_kernel(ctx_axis, heads, tokens, out_rows, scaling, places, *refs):
    blocks = refs[:ctx_axis]
    all_queries, all_grads, sent, keys, all_weights, all_score_grads, weights_sent, total, scores, upstream = refs[ctx_axis:]
    me = lax.axis_index("ctx")
    core = me & 1
    half_run = RUN // 2
    half = keys.shape[1]
    rank = all_grads.shape[1]
    width = blocks[0].shape[1]
    rows = RUN * heads

    total[...] = jnp.zeros_like(total)
    keys[:, :, width:] = jnp.zeros((2, half, keys.shape[2] - width), BF16)
    for far in range(ctx_axis):
        for run in range(tokens // RUN):
            rank_of_run = places[(me ^ far) * tokens + run * RUN] // RUN
            for sub in range(RUN // out_rows):
                group = (core ^ (sub & 1)) ^ 1
                start = pl.multiple_of(rank_of_run * half_run + (sub // 2) * out_rows, out_rows)
                piece = blocks[far][run * RUN + sub * out_rows : run * RUN + (sub + 1) * out_rows, :]
                keys[group, pl.ds(start, out_rows), :width] = piece

    @pl.loop(0, tokens // RUN)
    def _(step):
        own = pl.ds(pl.multiple_of(step * rows, rows), rows)
        queries, grads = all_queries.at[own], all_grads.at[own]
        weights_kept, score_grads = all_weights.at[step], all_score_grads.at[step]
        first = places[me * tokens + step * RUN]
        visible_steps = ((first // RUN) * half_run) // STEP + 1

        def run_of_queries(steps):
            seen = steps * STEP
            both = lambda columns: keys[:, :seen, :columns].reshape(2 * seen, columns)

            def multiply(tile):
                here = slice(tile * TILE, (tile + 1) * TILE)
                scores[tile % 2, : 2 * seen, :] = dot_nt(both(queries.shape[1]), queries[here, :])
                upstream[tile % 2, : 2 * seen, :] = dot_nt(both(rank), grads[here, :])

            def weigh(tile):
                here = slice(tile * TILE, (tile + 1) * TILE)
                score, up = scores.at[tile % 2], upstream.at[tile % 2]
                lanes = lax.broadcasted_iota(jnp.int32, (1, TILE), 1)
                query_places = first + ((lanes + tile * TILE) >> (heads.bit_length() - 1))
                index = lax.broadcasted_iota(jnp.int32, (STEP, 1), 0) + (steps - 1) * STEP
                peak = jnp.full((8, TILE), NEGATIVE, F32)
                for group in range(2):
                    for part in range(steps):
                        at = slice(group * seen + part * STEP, group * seen + (part + 1) * STEP)
                        value = score[at, :]
                        if part == steps - 1:
                            bit = core ^ (1 - group)
                            key_places = index + (index & ~(out_rows - 1)) + bit * out_rows
                            value = jnp.where(key_places <= query_places, value, NEGATIVE)
                            score[at, :] = value
                        peak = jnp.maximum(peak, jnp.max(value.reshape(STEP // 8, 8, TILE), axis=0))
                factor = scaling * math.log2(math.e)
                peak = jnp.max(peak, axis=0, keepdims=True) * factor
                sums = jnp.zeros((8, TILE), F32)
                mixed = jnp.zeros((8, TILE), F32)
                for part in range(2 * seen // PIECE):
                    at = slice(part * PIECE, (part + 1) * PIECE)
                    value = jnp.exp2(score[at, :] * factor - peak)
                    score[at, :] = value
                    sums += jnp.sum(value.reshape(PIECE // 8, 8, TILE), axis=0)
                    mixed += jnp.sum((value * up[at, :]).reshape(PIECE // 8, 8, TILE), axis=0)
                inverse = 1.0 / jnp.sum(sums, axis=0, keepdims=True)
                diagonal = jnp.sum(mixed, axis=0, keepdims=True) * inverse
                scaled = inverse * scaling
                for part in range(2 * seen // PIECE):
                    at = slice(part * PIECE, (part + 1) * PIECE)
                    group, row = (part * PIECE) // seen, (part * PIECE) % seen
                    to = slice(row, row + PIECE)
                    value = score[at, :]
                    weight = (value * inverse).astype(BF16)
                    if group == 0:
                        weights_sent[to, here] = weight
                    else:
                        weights_kept[to, here] = weight
                    grad = (value * scaled) * (up[at, :] - diagonal)
                    score_grads[group, to, here] = grad.astype(BF16)

            tiles = rows // TILE
            for tile in range(tiles):
                multiply(tile)
                weigh(tile)
            total[:seen, :] += dot_nn(score_grads[0, :seen, :], queries[...])
            total[:seen, :rank] += dot_nn(weights_sent[:seen, :], grads[...])
        for steps in range(1, half // STEP + 1):
            pl.when(visible_steps == steps)(functools.partial(run_of_queries, steps))

    place_rows(places, total, sent, 1 - core, ctx_axis)


def key_grad_kernel(ctx_axis, heads, tokens, places, weights, score_grads, queries, grads, kept, total):
    me = lax.axis_index("ctx")
    rank = grads.shape[1]
    half = total.shape[0]
    rows = RUN * heads
    total[...] = jnp.zeros_like(total)

    @pl.loop(0, tokens // RUN)
    def _(step):
        own = pl.ds(pl.multiple_of(step * rows, rows), rows)
        first = places[me * tokens + step * RUN]
        visible_steps = ((first // RUN) * (RUN // 2)) // STEP + 1

        def run_of_queries(steps):
            seen = steps * STEP
            total[:seen, :] += dot_nn(score_grads[step, 1, :seen, :], queries[own, :])
            total[:seen, :rank] += dot_nn(weights[step, :seen, :], grads[own, :])

        for steps in range(1, half // STEP + 1):
            pl.when(visible_steps == steps)(functools.partial(run_of_queries, steps))

    place_rows(places, total, kept, me & 1, ctx_axis)


def query_grad_kernel(heads, tokens, pieces, places, score_grads, keys, cosine, sine, *refs):
    before, refs = refs[:-5], refs[-5:]
    d_latent, d_rope, by_head, stage, done = refs
    me = lax.axis_index("ctx")
    rank, rope = stage.shape[1], cosine.shape[1]
    rows = RUN * heads
    span = TILE // heads
    to_heads = rows_to_heads(heads)

    def store(index):
        return pltpu.make_async_copy(
            stage.at[pl.ds(index * WIDE, WIDE)],
            d_latent.at[pl.ds(pieces[index] * WIDE, WIDE)],
            done.at[index],
        )

    def multiply(group, steps):
        seen = steps * STEP
        seen_keys = keys[:, :seen, :].reshape(2 * seen, keys.shape[2])
        for index in group:
            step, column = divmod(pieces[index] * WIDE, rows)
            grads = score_grads[step, :, :seen, column : column + WIDE].reshape(2 * seen, WIDE)
            value = dot_tn(grads, seen_keys)
            stage[index * WIDE : (index + 1) * WIDE, :] = value[:, :rank].astype(BF16)
            for tile in range(WIDE // TILE):
                here = slice(tile * TILE, (tile + 1) * TILE)
                start = (pieces[index] * WIDE + tile * TILE) // heads
                to = start - pieces[0] * WIDE // heads
                spread = lambda table: jnp.broadcast_to(
                    table[start : start + span, :][:, None, :], (span, heads, rope)
                ).reshape(TILE, rope)
                turned = value[here, rank : rank + rope]
                turned = (turned * spread(cosine) - half_turn_last(turned) * spread(sine)).astype(BF16)
                by_head[:, to : to + span, :] = dot_nn(to_heads, turned).reshape(heads, span, rope)

    for step in range(tokens // RUN):
        group = [index for index, piece in enumerate(pieces) if piece * WIDE // rows == step]
        if not group:
            continue
        first = places[me * tokens + step * RUN]
        visible_steps = ((first // RUN) * (RUN // 2)) // STEP + 1
        for steps in range(1, keys.shape[1] // STEP + 1):
            pl.when(visible_steps == steps)(functools.partial(multiply, group, steps))
        for index in group:
            store(index).start()
    if before:
        for head in range(heads):
            d_rope[head] = jnp.concatenate([before[1][head], by_head[head]], 0).T.astype(BF16)
    else:
        d_rope[...] = by_head[...]
    for index in range(len(pieces)):
        store(index).wait()


def pair_sum_kernel(kept, received, own, *others):
    own[...] = kept[0].astype(F32) + received[0].astype(F32)
    for chip, out in enumerate(others):
        out[...] = (kept[chip + 1].astype(F32) + received[chip + 1].astype(F32)).astype(BF16)


def plane_sum_kernel(own, *refs):
    head_axis = own.shape[0]
    received, kept, others = refs[: -head_axis], refs[-head_axis], refs[1 - head_axis :]
    mine = lax.axis_index("head")
    for far in range(head_axis):
        value = own[mine ^ far]
        for part in received:
            value += part[mine ^ far].astype(F32)
        if far == 0:
            kept[...] = value
        else:
            others[far - 1][...] = value.astype(BF16)


def head_sum_kernel(own, *refs):
    received, cosine, sine, d_latent, d_rope = refs[:-4], *refs[-4:]
    rank = d_latent.shape[1]
    value = own[...]
    for part in received:
        value += part[...].astype(F32)
    d_latent[...] = value[:, :rank]
    turned = value[:, rank:]
    d_rope[...] = turned * cosine[...] - half_turn_last(turned) * sine[...]


def pair(values, distance, axis):
    count = lax.axis_size(axis)
    return lax.ppermute(values, axis, [(i, i ^ distance) for i in range(count)])


def body(q_latent, q_rope, latent, rope_key, positions, d_out, w_uv):
    tokens, heads, rank = q_latent.shape
    rope = rope_key.shape[1]
    value_width = d_out.shape[2]
    sequence = positions.shape[0]
    head_axis, ctx_axis = lax.axis_size("head"), lax.axis_size("ctx")
    out_rows = sequence // (head_axis * ctx_axis)
    half = sequence // 2
    width = rank + rope
    padded = -(-width // 128) * 128
    rows = tokens * heads
    runs = tokens // RUN
    run_rows = RUN * heads
    scaling = (NOPE + rope) ** -0.5
    inverse = ROPE_BASE ** (-(np.arange(rope // 2, dtype=np.float64) / (rope // 2)))
    inverse = jnp.asarray(np.tile(inverse[:, None], (1, tokens)).astype(np.float32))

    def shape(*dims, dtype=BF16):
        return jax.ShapeDtypeStruct(dims, dtype)

    def cost(flops, nbytes, more=0):
        return pl.CostEstimate(flops=flops, bytes_accessed=nbytes, transcendentals=more)

    own_keys, tables = pl.pallas_call(
        functools.partial(key_kernel, head_axis, ctx_axis, out_rows),
        out_shape=(shape(tokens, width), shape(3, rope // 2, tokens, dtype=F32)),
        in_specs=[smem(), vmem(), vmem(), vmem()],
        out_specs=(vmem(),) * 2,
        compiler_params=params(60),
        cost_estimate=cost(8 << 30, 32 * MIB),
        name="own_keys",
    )(positions, latent, rope_key.T, inverse)

    blocks = [own_keys] + [None] * (ctx_axis - 1)
    for chip in range(1, ctx_axis // 2):
        blocks[2 * chip] = pair(own_keys, 2 * chip, "ctx")

    query_rows, grad_rows, own_cosine, own_sine, out_cosine, out_sine = pl.pallas_call(
        functools.partial(query_kernel, heads),
        out_shape=(shape(rows, padded), shape(rows, rank))
        + (shape(tokens, rope, dtype=F32),) * 2
        + (shape(out_rows, rope, dtype=F32),) * 2,
        in_specs=[vmem()] * 5,
        out_specs=(vmem(),) * 6,
        scratch_shapes=[
            pltpu.VMEM((heads, tokens, value_width), BF16),
            pltpu.VMEM((heads, tokens, width), BF16),
        ],
        compiler_params=params(24),
        cost_estimate=cost(2 * rows * rank * value_width, 10 * MIB),
        name="query_rows",
    )(
        q_latent.reshape(rows, rank),
        q_rope.transpose(1, 2, 0),
        d_out.reshape(rows, value_width),
        w_uv,
        tables,
    )

    blocks, query_rows, grad_rows = lax.optimization_barrier((blocks[::2], query_rows, grad_rows))
    blocks = [block for chip in blocks for block in (chip, pair(chip, 1, "ctx"))]

    slots = (ctx_axis // 2, head_axis, out_rows, width)
    sent, keys, weights_kept, score_grads = pl.pallas_call(
        functools.partial(front_kernel, ctx_axis, heads, tokens, out_rows, scaling),
        out_shape=(
            shape(*slots),
            shape(2, half, padded),
            shape(runs, half, run_rows),
            shape(runs, 2, half, run_rows),
        ),
        in_specs=[smem()] + [vmem()] * (ctx_axis + 2),
        out_specs=(vmem(),) * 4,
        scratch_shapes=[
            pltpu.VMEM((half, run_rows), BF16),
            pltpu.VMEM((half, padded), F32),
            pltpu.VMEM((2, sequence, TILE), F32),
            pltpu.VMEM((2, sequence, TILE), F32),
        ],
        compiler_params=params(30),
        cost_estimate=cost(7 * rows * sequence * width, 20 * MIB),
        name="front",
    )(positions, *blocks, query_rows, grad_rows)

    received = pair(sent, 1, "ctx")

    kept = pl.pallas_call(
        functools.partial(key_grad_kernel, ctx_axis, heads, tokens),
        out_shape=shape(*slots),
        in_specs=[smem()] + [vmem()] * 4,
        out_specs=vmem(),
        scratch_shapes=[pltpu.VMEM((half, padded), F32)],
        compiler_params=params(20),
        cost_estimate=cost(2 * rows * sequence * width, 10 * MIB),
        name="key_grad",
    )(positions, weights_kept, score_grads, query_rows, grad_rows)

    def small(kernel, outs, *operands):
        return pl.pallas_call(
            kernel,
            out_shape=outs,
            in_specs=[vmem()] * len(operands),
            out_specs=(vmem(),) * len(outs),
            compiler_params=params(4),
            name=kernel.__name__,
        )(*operands)

    low, high = shape(*slots[1:]), shape(*slots[1:], dtype=F32)
    own, *others = small(pair_sum_kernel, (high,) + (low,) * (slots[0] - 1), kept, received)
    others = [pair(part, 2 * (chip + 1), "ctx") for chip, part in enumerate(others)]

    anywhere = pl.BlockSpec(memory_space=pl.ANY)

    def query_grad(pieces, *before):
        part = shape(heads, len(pieces) * WIDE // heads, rope, dtype=F32)
        return pl.pallas_call(
            functools.partial(query_grad_kernel, heads, tokens, pieces),
            out_shape=(shape(rows, rank), shape(heads, rope, tokens) if before else part),
            in_specs=[smem()] + [vmem()] * 4 + [anywhere, vmem()] * bool(before),
            out_specs=(anywhere, vmem()),
            input_output_aliases={5: 0} if before else {},
            scratch_shapes=[
                pltpu.VMEM(part.shape, F32),
                pltpu.VMEM((len(pieces) * WIDE, rank), BF16),
                pltpu.SemaphoreType.DMA((len(pieces),)),
            ],
            compiler_params=params(20),
            cost_estimate=cost(2 * len(pieces) * WIDE * sequence * width, 5 * MIB),
            name="query_grad",
        )(positions, score_grads, keys, own_cosine, own_sine, *before)

    pieces = range(rows // WIDE)
    d_q_latent, turned = query_grad(pieces[:-1])
    others, d_q_latent, turned = lax.optimization_barrier((others, d_q_latent, turned))
    low, high = shape(*slots[2:]), shape(*slots[2:], dtype=F32)
    own, *others = small(plane_sum_kernel, (high,) + (low,) * (head_axis - 1), own, *others)
    others, d_q_latent, turned = lax.optimization_barrier((others, d_q_latent, turned))
    others = [pair(part, far + 1, "head") for far, part in enumerate(others)]
    d_q_latent, d_q_rope = query_grad(pieces[-1:], d_q_latent, turned)
    others, d_q_latent, d_q_rope = lax.optimization_barrier((others, d_q_latent, d_q_rope))
    d_latent, d_rope_key = small(
        head_sum_kernel,
        (shape(out_rows, rank, dtype=F32), shape(out_rows, rope, dtype=F32)),
        own,
        *others,
        out_cosine,
        out_sine,
    )
    return (
        d_q_latent.reshape(tokens, heads, rank),
        d_q_rope.transpose(2, 0, 1),
        d_latent,
        d_rope_key,
    )


def solution(mesh):
    placed = (
        P("ctx", "head", None),
        P("ctx", "head", None),
        P("ctx", None),
        P("ctx", None),
        P(),
        P("ctx", "head", None),
        P("head", None, None),
    )
    return jax.shard_map(
        body,
        mesh=mesh,
        in_specs=placed,
        out_specs=(
            P("ctx", "head", None),
            P("ctx", "head", None),
            P(("head", "ctx"), None),
            P(("head", "ctx"), None),
        ),
        check_vma=False,
    )
```

```python
import functools
import math

import jax
import jax.numpy as jnp
import numpy as np
from jax import lax
from jax.experimental import pallas as pl
from jax.experimental.pallas import tpu as pltpu
from jax.sharding import PartitionSpec as P

NOPE = 128
RUN = 64
TILE = 256
PIECE = 64
WIDE = 512
STEP = 128
ROPE_BASE = 10000.0
NEGATIVE = -1e30
MIB = 1 << 20
BF16 = jnp.bfloat16
F32 = jnp.float32


def dot_nn(left, right):
    return lax.dot_general(left, right, (((1,), (0,)), ((), ())), preferred_element_type=F32)


def dot_nt(left, right):
    return lax.dot_general(left, right, (((1,), (1,)), ((), ())), preferred_element_type=F32)


def dot_tn(left, right):
    return lax.dot_general(left, right, (((0,), (0,)), ((), ())), preferred_element_type=F32)


def half_turn(values):
    middle = values.shape[0] // 2
    return jnp.concatenate([-values[middle:], values[:middle]], 0)


def half_turn_last(values):
    middle = values.shape[-1] // 2
    return jnp.concatenate([-values[..., middle:], values[..., :middle]], -1)


def vmem():
    return pl.BlockSpec(memory_space=pltpu.VMEM)


def smem():
    return pl.BlockSpec(memory_space=pltpu.SMEM)


def params(mib):
    return pltpu.CompilerParams(vmem_limit_bytes=mib * MIB)


def twice(values):
    return jnp.concatenate([values, values], 0)


def key_kernel(head_axis, ctx_axis, out_rows, places, latent, rope, inverse, keys, tables):
    me = lax.axis_index("ctx")
    tokens, rank = latent.shape
    lanes = lax.broadcasted_iota(jnp.int32, inverse.shape, 1)
    count = lanes
    for run in range(tokens // RUN):
        first = places[me * tokens + run * RUN] - run * RUN
        count = jnp.where((lanes >> (RUN.bit_length() - 1)) == run, lanes + first, count)
    angles = count.astype(F32) * inverse[...]
    cosine, sine = jnp.cos(angles), jnp.sin(angles)
    values = rope[...].astype(F32)
    turned = values * twice(cosine) + half_turn(values) * twice(sine)
    keys[:, :rank] = latent[...]
    keys[:, rank:] = turned.T.astype(BF16)
    first = places[(lax.axis_index("head") * ctx_axis + me) * out_rows]
    tables[0] = cosine
    tables[1] = sine
    tables[2] = (lanes + first).astype(F32) * inverse[...]


def rows_to_heads(heads):
    span = TILE // heads
    shift_span, shift_heads = span.bit_length() - 1, heads.bit_length() - 1
    by_row = lax.broadcasted_iota(jnp.int32, (TILE, TILE), 0)
    by_column = lax.broadcasted_iota(jnp.int32, (TILE, TILE), 1)
    same = ((by_row >> shift_span) == (by_column & (heads - 1))) & (
        (by_row & (span - 1)) == (by_column >> shift_heads)
    )
    return jnp.where(same, 1.0, 0.0).astype(BF16)


def query_kernel(heads, q_latent, q_rope, d_out, w_uv, tables, *refs):
    queries, grads, own_cosine, own_sine, out_cosine, out_sine, by_head, grad_heads = refs
    cosine, sine = twice(tables[0]), twice(tables[1])
    own_cosine[...] = cosine.T
    own_sine[...] = sine.T
    out_cosine[...] = twice(jnp.cos(tables[2])).T[: out_cosine.shape[0], :]
    out_sine[...] = twice(jnp.sin(tables[2])).T[: out_sine.shape[0], :]
    rows, rank = q_latent.shape
    rope = q_rope.shape[1]
    span = TILE // heads
    to_heads = rows_to_heads(heads)
    tiles = rows // TILE
    queries[:, :rank] = q_latent[...]
    queries[:, rank + rope :] = jnp.zeros((rows, queries.shape[1] - rank - rope), BF16)
    for tile in range(tiles):
        here = slice(tile * TILE, (tile + 1) * TILE)
        own = slice(tile * span, (tile + 1) * span)
        by_head[:, own, :] = dot_nn(to_heads, d_out[here, :]).astype(BF16).reshape(heads, span, d_out.shape[1])
    for head in range(heads):
        grad_heads[head, :, :rank] = dot_nt(by_head[head], w_uv[head]).astype(BF16)
        values = q_rope[head].astype(F32)
        turned = values * cosine + half_turn(values) * sine
        grad_heads[head, :, rank:] = turned.T.astype(BF16)
    for tile in range(tiles):
        here = slice(tile * TILE, (tile + 1) * TILE)
        own = slice(tile * span, (tile + 1) * span)
        block = grad_heads[:, own, :].reshape(TILE, rank + rope)
        block = dot_tn(to_heads, block).astype(BF16)
        grads[here, :] = block[:, :rank]
        queries[here, rank : rank + rope] = block[:, rank:]


def place_rows(places, total, out, core, ctx_axis):
    out_rows, width = out.shape[2], out.shape[3]
    chip = lax.axis_index("ctx") >> 1
    half_run = RUN // 2
    for run in range(places.shape[0] // RUN):
        rank_of_run = places[run * RUN] // RUN
        for piece in range(half_run // out_rows):
            block = run * (RUN // out_rows) + 2 * piece
            source = pl.ds(pl.multiple_of(rank_of_run * half_run + piece * out_rows, out_rows), out_rows)
            slot = ((block % ctx_axis) >> 1) ^ chip
            out[slot, block // ctx_axis] = total[source, :width].astype(out.dtype)


def front_kernel(ctx_axis, heads, tokens, out_rows, scaling, places, *refs):
    blocks = refs[:ctx_axis]
    all_queries, all_grads, sent, keys, all_weights, all_score_grads, weights_sent, total, scores, upstream = refs[ctx_axis:]
    me = lax.axis_index("ctx")
    core = me & 1
    half_run = RUN // 2
    half = keys.shape[1]
    rank = all_grads.shape[1]
    width = blocks[0].shape[1]
    rows = RUN * heads

    total[...] = jnp.zeros_like(total)
    keys[:, :, width:] = jnp.zeros((2, half, keys.shape[2] - width), BF16)
    for far in range(ctx_axis):
        for run in range(tokens // RUN):
            rank_of_run = places[(me ^ far) * tokens + run * RUN] // RUN
            for sub in range(RUN // out_rows):
                group = (core ^ (sub & 1)) ^ 1
                start = pl.multiple_of(rank_of_run * half_run + (sub // 2) * out_rows, out_rows)
                piece = blocks[far][run * RUN + sub * out_rows : run * RUN + (sub + 1) * out_rows, :]
                keys[group, pl.ds(start, out_rows), :width] = piece

    @pl.loop(0, tokens // RUN)
    def _(step):
        own = pl.ds(pl.multiple_of(step * rows, rows), rows)
        queries, grads = all_queries.at[own], all_grads.at[own]
        weights_kept, score_grads = all_weights.at[step], all_score_grads.at[step]
        first = places[me * tokens + step * RUN]
        visible_steps = ((first // RUN) * half_run) // STEP + 1

        def run_of_queries(steps):
            seen = steps * STEP
            both = lambda columns: keys[:, :seen, :columns].reshape(2 * seen, columns)

            def multiply(tile):
                here = slice(tile * TILE, (tile + 1) * TILE)
                scores[tile % 2, : 2 * seen, :] = dot_nt(both(queries.shape[1]), queries[here, :])
                upstream[tile % 2, : 2 * seen, :] = dot_nt(both(rank), grads[here, :])

            def weigh(tile):
                here = slice(tile * TILE, (tile + 1) * TILE)
                score, up = scores.at[tile % 2], upstream.at[tile % 2]
                lanes = lax.broadcasted_iota(jnp.int32, (1, TILE), 1)
                query_places = first + ((lanes + tile * TILE) >> (heads.bit_length() - 1))
                index = lax.broadcasted_iota(jnp.int32, (STEP, 1), 0) + (steps - 1) * STEP
                peak = jnp.full((8, TILE), NEGATIVE, F32)
                for group in range(2):
                    for part in range(steps):
                        at = slice(group * seen + part * STEP, group * seen + (part + 1) * STEP)
                        value = score[at, :]
                        if part == steps - 1:
                            bit = core ^ (1 - group)
                            key_places = index + (index & ~(out_rows - 1)) + bit * out_rows
                            value = jnp.where(key_places <= query_places, value, NEGATIVE)
                            score[at, :] = value
                        peak = jnp.maximum(peak, jnp.max(value.reshape(STEP // 8, 8, TILE), axis=0))
                factor = scaling * math.log2(math.e)
                peak = jnp.max(peak, axis=0, keepdims=True) * factor
                sums = jnp.zeros((8, TILE), F32)
                mixed = jnp.zeros((8, TILE), F32)
                for part in range(2 * seen // PIECE):
                    at = slice(part * PIECE, (part + 1) * PIECE)
                    value = jnp.exp2(score[at, :] * factor - peak)
                    score[at, :] = value
                    sums += jnp.sum(value.reshape(PIECE // 8, 8, TILE), axis=0)
                    mixed += jnp.sum((value * up[at, :]).reshape(PIECE // 8, 8, TILE), axis=0)
                inverse = 1.0 / jnp.sum(sums, axis=0, keepdims=True)
                diagonal = jnp.sum(mixed, axis=0, keepdims=True) * inverse
                scaled = inverse * scaling
                for part in range(2 * seen // PIECE):
                    at = slice(part * PIECE, (part + 1) * PIECE)
                    group, row = (part * PIECE) // seen, (part * PIECE) % seen
                    to = slice(row, row + PIECE)
                    value = score[at, :]
                    weight = (value * inverse).astype(BF16)
                    if group == 0:
                        weights_sent[to, here] = weight
                    else:
                        weights_kept[to, here] = weight
                    grad = (value * scaled) * (up[at, :] - diagonal)
                    score_grads[group, to, here] = grad.astype(BF16)

            tiles = rows // TILE
            for tile in range(tiles):
                multiply(tile)
                weigh(tile)
            total[:seen, :] += dot_nn(score_grads[0, :seen, :], queries[...])
            total[:seen, :rank] += dot_nn(weights_sent[:seen, :], grads[...])
        for steps in range(1, half // STEP + 1):
            pl.when(visible_steps == steps)(functools.partial(run_of_queries, steps))

    place_rows(places, total, sent, 1 - core, ctx_axis)


def key_grad_kernel(ctx_axis, heads, tokens, places, weights, score_grads, queries, grads, kept, total):
    me = lax.axis_index("ctx")
    rank = grads.shape[1]
    half = total.shape[0]
    rows = RUN * heads
    total[...] = jnp.zeros_like(total)

    @pl.loop(0, tokens // RUN)
    def _(step):
        own = pl.ds(pl.multiple_of(step * rows, rows), rows)
        first = places[me * tokens + step * RUN]
        visible_steps = ((first // RUN) * (RUN // 2)) // STEP + 1

        def run_of_queries(steps):
            seen = steps * STEP
            total[:seen, :] += dot_nn(score_grads[step, 1, :seen, :], queries[own, :])
            total[:seen, :rank] += dot_nn(weights[step, :seen, :], grads[own, :])

        for steps in range(1, half // STEP + 1):
            pl.when(visible_steps == steps)(functools.partial(run_of_queries, steps))

    place_rows(places, total, kept, me & 1, ctx_axis)


def query_grad_kernel(heads, tokens, pieces, places, score_grads, keys, cosine, sine, *refs):
    before, refs = refs[:-5], refs[-5:]
    d_latent, d_rope, by_head, stage, done = refs
    me = lax.axis_index("ctx")
    rank, rope = stage.shape[1], cosine.shape[1]
    rows = RUN * heads
    span = TILE // heads
    to_heads = rows_to_heads(heads)

    def store(index):
        return pltpu.make_async_copy(
            stage.at[pl.ds(index * WIDE, WIDE)],
            d_latent.at[pl.ds(pieces[index] * WIDE, WIDE)],
            done.at[index],
        )

    def multiply(group, steps):
        seen = steps * STEP
        seen_keys = keys[:, :seen, :].reshape(2 * seen, keys.shape[2])
        for index in group:
            step, column = divmod(pieces[index] * WIDE, rows)
            grads = score_grads[step, :, :seen, column : column + WIDE].reshape(2 * seen, WIDE)
            value = dot_tn(grads, seen_keys)
            stage[index * WIDE : (index + 1) * WIDE, :] = value[:, :rank].astype(BF16)
            for tile in range(WIDE // TILE):
                here = slice(tile * TILE, (tile + 1) * TILE)
                start = (pieces[index] * WIDE + tile * TILE) // heads
                to = start - pieces[0] * WIDE // heads
                spread = lambda table: jnp.broadcast_to(
                    table[start : start + span, :][:, None, :], (span, heads, rope)
                ).reshape(TILE, rope)
                turned = value[here, rank : rank + rope]
                turned = (turned * spread(cosine) - half_turn_last(turned) * spread(sine)).astype(BF16)
                by_head[:, to : to + span, :] = dot_nn(to_heads, turned).reshape(heads, span, rope)

    for step in range(tokens // RUN):
        group = [index for index, piece in enumerate(pieces) if piece * WIDE // rows == step]
        if not group:
            continue
        first = places[me * tokens + step * RUN]
        visible_steps = ((first // RUN) * (RUN // 2)) // STEP + 1
        for steps in range(1, keys.shape[1] // STEP + 1):
            pl.when(visible_steps == steps)(functools.partial(multiply, group, steps))
        for index in group:
            store(index).start()
    if before:
        for head in range(heads):
            d_rope[head] = jnp.concatenate([before[1][head], by_head[head]], 0).T.astype(BF16)
    else:
        d_rope[...] = by_head[...]
    for index in range(len(pieces)):
        store(index).wait()


def pair_sum_kernel(kept, received, own, *others):
    own[...] = kept[0].astype(F32) + received[0].astype(F32)
    for chip, out in enumerate(others):
        out[...] = (kept[chip + 1].astype(F32) + received[chip + 1].astype(F32)).astype(BF16)


def plane_sum_kernel(own, *refs):
    head_axis = own.shape[0]
    received, kept, others = refs[: -head_axis], refs[-head_axis], refs[1 - head_axis :]
    mine = lax.axis_index("head")
    for far in range(head_axis):
        value = own[mine ^ far]
        for part in received:
            value += part[mine ^ far].astype(F32)
        if far == 0:
            kept[...] = value
        else:
            others[far - 1][...] = value.astype(BF16)


def head_sum_kernel(own, *refs):
    received, cosine, sine, d_latent, d_rope = refs[:-4], *refs[-4:]
    rank = d_latent.shape[1]
    value = own[...]
    for part in received:
        value += part[...].astype(F32)
    d_latent[...] = value[:, :rank]
    turned = value[:, rank:]
    d_rope[...] = turned * cosine[...] - half_turn_last(turned) * sine[...]


def pair(values, distance, axis):
    count = lax.axis_size(axis)
    return lax.ppermute(values, axis, [(i, i ^ distance) for i in range(count)])


def body(q_latent, q_rope, latent, rope_key, positions, d_out, w_uv):
    tokens, heads, rank = q_latent.shape
    rope = rope_key.shape[1]
    value_width = d_out.shape[2]
    sequence = positions.shape[0]
    head_axis, ctx_axis = lax.axis_size("head"), lax.axis_size("ctx")
    out_rows = sequence // (head_axis * ctx_axis)
    half = sequence // 2
    width = rank + rope
    padded = -(-width // 128) * 128
    rows = tokens * heads
    runs = tokens // RUN
    run_rows = RUN * heads
    scaling = (NOPE + rope) ** -0.5
    inverse = ROPE_BASE ** (-(np.arange(rope // 2, dtype=np.float64) / (rope // 2)))
    inverse = jnp.asarray(np.tile(inverse[:, None], (1, tokens)).astype(np.float32))

    def shape(*dims, dtype=BF16):
        return jax.ShapeDtypeStruct(dims, dtype)

    def cost(flops, nbytes, more=0):
        return pl.CostEstimate(flops=flops, bytes_accessed=nbytes, transcendentals=more)

    own_keys, tables = pl.pallas_call(
        functools.partial(key_kernel, head_axis, ctx_axis, out_rows),
        out_shape=(shape(tokens, width), shape(3, rope // 2, tokens, dtype=F32)),
        in_specs=[smem(), vmem(), vmem(), vmem()],
        out_specs=(vmem(),) * 2,
        compiler_params=params(58),
        cost_estimate=cost(8 << 30, 32 * MIB),
        name="own_keys",
    )(positions, latent, rope_key.T, inverse)

    blocks = [own_keys] + [None] * (ctx_axis - 1)
    for chip in range(1, ctx_axis // 2):
        blocks[2 * chip] = pair(own_keys, 2 * chip, "ctx")

    query_rows, grad_rows, own_cosine, own_sine, out_cosine, out_sine = pl.pallas_call(
        functools.partial(query_kernel, heads),
        out_shape=(shape(rows, padded), shape(rows, rank))
        + (shape(tokens, rope, dtype=F32),) * 2
        + (shape(out_rows, rope, dtype=F32),) * 2,
        in_specs=[vmem()] * 5,
        out_specs=(vmem(),) * 6,
        scratch_shapes=[
            pltpu.VMEM((heads, tokens, value_width), BF16),
            pltpu.VMEM((heads, tokens, width), BF16),
        ],
        compiler_params=params(24),
        cost_estimate=cost(2 * rows * rank * value_width, 10 * MIB),
        name="query_rows",
    )(
        q_latent.reshape(rows, rank),
        q_rope.transpose(1, 2, 0),
        d_out.reshape(rows, value_width),
        w_uv,
        tables,
    )

    blocks, query_rows, grad_rows = lax.optimization_barrier((blocks[::2], query_rows, grad_rows))
    blocks = [block for chip in blocks for block in (chip, pair(chip, 1, "ctx"))]

    slots = (ctx_axis // 2, head_axis, out_rows, width)
    sent, keys, weights_kept, score_grads = pl.pallas_call(
        functools.partial(front_kernel, ctx_axis, heads, tokens, out_rows, scaling),
        out_shape=(
            shape(*slots),
            shape(2, half, padded),
            shape(runs, half, run_rows),
            shape(runs, 2, half, run_rows),
        ),
        in_specs=[smem()] + [vmem()] * (ctx_axis + 2),
        out_specs=(vmem(),) * 4,
        scratch_shapes=[
            pltpu.VMEM((half, run_rows), BF16),
            pltpu.VMEM((half, padded), F32),
            pltpu.VMEM((2, sequence, TILE), F32),
            pltpu.VMEM((2, sequence, TILE), F32),
        ],
        compiler_params=params(30),
        cost_estimate=cost(7 * rows * sequence * width, 20 * MIB),
        name="front",
    )(positions, *blocks, query_rows, grad_rows)

    received = pair(sent, 1, "ctx")

    kept = pl.pallas_call(
        functools.partial(key_grad_kernel, ctx_axis, heads, tokens),
        out_shape=shape(*slots),
        in_specs=[smem()] + [vmem()] * 4,
        out_specs=vmem(),
        scratch_shapes=[pltpu.VMEM((half, padded), F32)],
        compiler_params=params(20),
        cost_estimate=cost(2 * rows * sequence * width, 10 * MIB),
        name="key_grad",
    )(positions, weights_kept, score_grads, query_rows, grad_rows)

    def small(kernel, outs, *operands):
        return pl.pallas_call(
            kernel,
            out_shape=outs,
            in_specs=[vmem()] * len(operands),
            out_specs=(vmem(),) * len(outs),
            compiler_params=params(4),
            name=kernel.__name__,
        )(*operands)

    low, high = shape(*slots[1:]), shape(*slots[1:], dtype=F32)
    own, *others = small(pair_sum_kernel, (high,) + (low,) * (slots[0] - 1), kept, received)
    others = [pair(part, 2 * (chip + 1), "ctx") for chip, part in reversed(list(enumerate(others)))]

    anywhere = pl.BlockSpec(memory_space=pl.ANY)

    def query_grad(pieces, *before):
        part = shape(heads, len(pieces) * WIDE // heads, rope, dtype=F32)
        return pl.pallas_call(
            functools.partial(query_grad_kernel, heads, tokens, pieces),
            out_shape=(shape(rows, rank), shape(heads, rope, tokens) if before else part),
            in_specs=[smem()] + [vmem()] * 4 + [anywhere, vmem()] * bool(before),
            out_specs=(anywhere, vmem()),
            input_output_aliases={5: 0} if before else {},
            scratch_shapes=[
                pltpu.VMEM(part.shape, F32),
                pltpu.VMEM((len(pieces) * WIDE, rank), BF16),
                pltpu.SemaphoreType.DMA((len(pieces),)),
            ],
            compiler_params=params(20),
            cost_estimate=cost(2 * len(pieces) * WIDE * sequence * width, 5 * MIB),
            name="query_grad",
        )(positions, score_grads, keys, own_cosine, own_sine, *before)

    pieces = range(rows // WIDE)
    d_q_latent, turned = query_grad(pieces[:-1])
    others, d_q_latent, turned = lax.optimization_barrier((others, d_q_latent, turned))
    low, high = shape(*slots[2:]), shape(*slots[2:], dtype=F32)
    own, *others = small(plane_sum_kernel, (high,) + (low,) * (head_axis - 1), own, *others)
    others, d_q_latent, turned = lax.optimization_barrier((others, d_q_latent, turned))
    others = [pair(part, far + 1, "head") for far, part in reversed(list(enumerate(others)))]
    d_q_latent, d_q_rope = query_grad(pieces[-1:], d_q_latent, turned)
    others, d_q_latent, d_q_rope = lax.optimization_barrier((others, d_q_latent, d_q_rope))
    d_latent, d_rope_key = small(
        head_sum_kernel,
        (shape(out_rows, rank, dtype=F32), shape(out_rows, rope, dtype=F32)),
        own,
        *others,
        out_cosine,
        out_sine,
    )
    return (
        d_q_latent.reshape(tokens, heads, rank),
        d_q_rope.transpose(2, 0, 1),
        d_latent,
        d_rope_key,
    )


def solution(mesh):
    placed = (
        P("ctx", "head", None),
        P("ctx", "head", None),
        P("ctx", None),
        P("ctx", None),
        P(),
        P("ctx", "head", None),
        P("head", None, None),
    )
    return jax.shard_map(
        body,
        mesh=mesh,
        in_specs=placed,
        out_specs=(
            P("ctx", "head", None),
            P("ctx", "head", None),
            P(("head", "ctx"), None),
            P(("head", "ctx"), None),
        ),
        check_vma=False,
    )
```

```python
import functools
import math

import jax
import jax.numpy as jnp
import numpy as np
from jax import lax
from jax.experimental import pallas as pl
from jax.experimental.pallas import tpu as pltpu
from jax.sharding import PartitionSpec as P

NOPE = 128
RUN = 64
TILE = 256
PIECE = 64
WIDE = 512
STEP = 64
ROPE_BASE = 10000.0
NEGATIVE = -1e30
MIB = 1 << 20
BF16 = jnp.bfloat16
F32 = jnp.float32


def dot_nn(left, right):
    return lax.dot_general(left, right, (((1,), (0,)), ((), ())), preferred_element_type=F32)


def dot_nt(left, right):
    return lax.dot_general(left, right, (((1,), (1,)), ((), ())), preferred_element_type=F32)


def dot_tn(left, right):
    return lax.dot_general(left, right, (((0,), (0,)), ((), ())), preferred_element_type=F32)


def half_turn(values):
    middle = values.shape[0] // 2
    return jnp.concatenate([-values[middle:], values[:middle]], 0)


def half_turn_last(values):
    middle = values.shape[-1] // 2
    return jnp.concatenate([-values[..., middle:], values[..., :middle]], -1)


def vmem():
    return pl.BlockSpec(memory_space=pltpu.VMEM)


def smem():
    return pl.BlockSpec(memory_space=pltpu.SMEM)


def params(mib):
    return pltpu.CompilerParams(vmem_limit_bytes=mib * MIB)


def twice(values):
    return jnp.concatenate([values, values], 0)


def key_kernel(head_axis, ctx_axis, out_rows, places, latent, rope, inverse, keys, tables):
    me = lax.axis_index("ctx")
    tokens, rank = latent.shape
    lanes = lax.broadcasted_iota(jnp.int32, inverse.shape, 1)
    count = lanes
    for run in range(tokens // RUN):
        first = places[me * tokens + run * RUN] - run * RUN
        count = jnp.where((lanes >> (RUN.bit_length() - 1)) == run, lanes + first, count)
    angles = count.astype(F32) * inverse[...]
    cosine, sine = jnp.cos(angles), jnp.sin(angles)
    values = rope[...].astype(F32)
    turned = values * twice(cosine) + half_turn(values) * twice(sine)
    keys[:, :rank] = latent[...]
    keys[:, rank:] = turned.T.astype(BF16)
    first = places[(lax.axis_index("head") * ctx_axis + me) * out_rows]
    tables[0] = cosine
    tables[1] = sine
    tables[2] = (lanes + first).astype(F32) * inverse[...]


def rows_to_heads(heads):
    span = TILE // heads
    shift_span, shift_heads = span.bit_length() - 1, heads.bit_length() - 1
    by_row = lax.broadcasted_iota(jnp.int32, (TILE, TILE), 0)
    by_column = lax.broadcasted_iota(jnp.int32, (TILE, TILE), 1)
    same = ((by_row >> shift_span) == (by_column & (heads - 1))) & (
        (by_row & (span - 1)) == (by_column >> shift_heads)
    )
    return jnp.where(same, 1.0, 0.0).astype(BF16)


def query_kernel(heads, q_latent, q_rope, d_out, w_uv, tables, *refs):
    queries, grads, own_cosine, own_sine, out_cosine, out_sine, by_head, grad_heads = refs
    cosine, sine = twice(tables[0]), twice(tables[1])
    own_cosine[...] = cosine.T
    own_sine[...] = sine.T
    out_cosine[...] = twice(jnp.cos(tables[2])).T[: out_cosine.shape[0], :]
    out_sine[...] = twice(jnp.sin(tables[2])).T[: out_sine.shape[0], :]
    rows, rank = q_latent.shape
    rope = q_rope.shape[1]
    span = TILE // heads
    to_heads = rows_to_heads(heads)
    tiles = rows // TILE
    queries[:, :rank] = q_latent[...]
    queries[:, rank + rope :] = jnp.zeros((rows, queries.shape[1] - rank - rope), BF16)
    for tile in range(tiles):
        here = slice(tile * TILE, (tile + 1) * TILE)
        own = slice(tile * span, (tile + 1) * span)
        by_head[:, own, :] = dot_nn(to_heads, d_out[here, :]).astype(BF16).reshape(heads, span, d_out.shape[1])
    for head in range(heads):
        grad_heads[head, :, :rank] = dot_nt(by_head[head], w_uv[head]).astype(BF16)
        values = q_rope[head].astype(F32)
        turned = values * cosine + half_turn(values) * sine
        grad_heads[head, :, rank:] = turned.T.astype(BF16)
    for tile in range(tiles):
        here = slice(tile * TILE, (tile + 1) * TILE)
        own = slice(tile * span, (tile + 1) * span)
        block = grad_heads[:, own, :].reshape(TILE, rank + rope)
        block = dot_tn(to_heads, block).astype(BF16)
        grads[here, :] = block[:, :rank]
        queries[here, rank : rank + rope] = block[:, rank:]


def place_rows(places, total, out, core, ctx_axis):
    out_rows, width = out.shape[2], out.shape[3]
    chip = lax.axis_index("ctx") >> 1
    half_run = RUN // 2
    for run in range(places.shape[0] // RUN):
        rank_of_run = places[run * RUN] // RUN
        for piece in range(half_run // out_rows):
            block = run * (RUN // out_rows) + 2 * piece
            source = pl.ds(pl.multiple_of(rank_of_run * half_run + piece * out_rows, out_rows), out_rows)
            slot = ((block % ctx_axis) >> 1) ^ chip
            out[slot, block // ctx_axis] = total[source, :width].astype(out.dtype)


def front_kernel(ctx_axis, heads, tokens, out_rows, scaling, places, *refs):
    blocks = refs[:ctx_axis]
    all_queries, all_grads, sent, keys, all_weights, all_score_grads, weights_sent, total, scores, upstream = refs[ctx_axis:]
    me = lax.axis_index("ctx")
    core = me & 1
    half_run = RUN // 2
    half = keys.shape[1]
    rank = all_grads.shape[1]
    width = blocks[0].shape[1]
    rows = RUN * heads

    total[...] = jnp.zeros_like(total)
    keys[:, :, width:] = jnp.zeros((2, half, keys.shape[2] - width), BF16)
    for far in range(ctx_axis):
        for run in range(tokens // RUN):
            rank_of_run = places[(me ^ far) * tokens + run * RUN] // RUN
            for sub in range(RUN // out_rows):
                group = (core ^ (sub & 1)) ^ 1
                start = pl.multiple_of(rank_of_run * half_run + (sub // 2) * out_rows, out_rows)
                piece = blocks[far][run * RUN + sub * out_rows : run * RUN + (sub + 1) * out_rows, :]
                keys[group, pl.ds(start, out_rows), :width] = piece

    @pl.loop(0, tokens // RUN)
    def _(step):
        own = pl.ds(pl.multiple_of(step * rows, rows), rows)
        queries, grads = all_queries.at[own], all_grads.at[own]
        weights_kept, score_grads = all_weights.at[step], all_score_grads.at[step]
        first = places[me * tokens + step * RUN]
        visible_steps = ((first // RUN) * half_run) // STEP + 1

        def run_of_queries(steps):
            seen = steps * STEP
            both = lambda columns: keys[:, :seen, :columns].reshape(2 * seen, columns)

            def multiply(tile):
                here = slice(tile * TILE, (tile + 1) * TILE)
                scores[tile % 2, : 2 * seen, :] = dot_nt(both(queries.shape[1]), queries[here, :])
                upstream[tile % 2, : 2 * seen, :] = dot_nt(both(rank), grads[here, :])

            def weigh(tile):
                here = slice(tile * TILE, (tile + 1) * TILE)
                score, up = scores.at[tile % 2], upstream.at[tile % 2]
                lanes = lax.broadcasted_iota(jnp.int32, (1, TILE), 1)
                query_places = first + ((lanes + tile * TILE) >> (heads.bit_length() - 1))
                index = lax.broadcasted_iota(jnp.int32, (STEP, 1), 0) + (steps - 1) * STEP
                peak = jnp.full((8, TILE), NEGATIVE, F32)
                for group in range(2):
                    for part in range(steps):
                        at = slice(group * seen + part * STEP, group * seen + (part + 1) * STEP)
                        value = score[at, :]
                        if part == steps - 1:
                            bit = core ^ (1 - group)
                            key_places = index + (index & ~(out_rows - 1)) + bit * out_rows
                            value = jnp.where(key_places <= query_places, value, NEGATIVE)
                            score[at, :] = value
                        peak = jnp.maximum(peak, jnp.max(value.reshape(STEP // 8, 8, TILE), axis=0))
                factor = scaling * math.log2(math.e)
                peak = jnp.max(peak, axis=0, keepdims=True) * factor
                sums = jnp.zeros((8, TILE), F32)
                mixed = jnp.zeros((8, TILE), F32)
                for part in range(2 * seen // PIECE):
                    at = slice(part * PIECE, (part + 1) * PIECE)
                    value = jnp.exp2(score[at, :] * factor - peak)
                    score[at, :] = value
                    sums += jnp.sum(value.reshape(PIECE // 8, 8, TILE), axis=0)
                    mixed += jnp.sum((value * up[at, :]).reshape(PIECE // 8, 8, TILE), axis=0)
                inverse = 1.0 / jnp.sum(sums, axis=0, keepdims=True)
                diagonal = jnp.sum(mixed, axis=0, keepdims=True) * inverse
                scaled = inverse * scaling
                for part in range(2 * seen // PIECE):
                    at = slice(part * PIECE, (part + 1) * PIECE)
                    group, row = (part * PIECE) // seen, (part * PIECE) % seen
                    to = slice(row, row + PIECE)
                    value = score[at, :]
                    weight = (value * inverse).astype(BF16)
                    if group == 0:
                        weights_sent[to, here] = weight
                    else:
                        weights_kept[to, here] = weight
                    grad = (value * scaled) * (up[at, :] - diagonal)
                    score_grads[group, to, here] = grad.astype(BF16)

            tiles = rows // TILE
            for tile in range(tiles):
                multiply(tile)
                weigh(tile)
            total[:seen, :] += dot_nn(score_grads[0, :seen, :], queries[...])
            total[:seen, :rank] += dot_nn(weights_sent[:seen, :], grads[...])
        for steps in range(1, half // STEP + 1):
            pl.when(visible_steps == steps)(functools.partial(run_of_queries, steps))

    place_rows(places, total, sent, 1 - core, ctx_axis)


def key_grad_kernel(ctx_axis, heads, tokens, places, weights, score_grads, queries, grads, kept, total):
    me = lax.axis_index("ctx")
    rank = grads.shape[1]
    half = total.shape[0]
    rows = RUN * heads
    total[...] = jnp.zeros_like(total)

    @pl.loop(0, tokens // RUN)
    def _(step):
        own = pl.ds(pl.multiple_of(step * rows, rows), rows)
        first = places[me * tokens + step * RUN]
        visible_steps = ((first // RUN) * (RUN // 2)) // STEP + 1

        def run_of_queries(steps):
            seen = steps * STEP
            total[:seen, :] += dot_nn(score_grads[step, 1, :seen, :], queries[own, :])
            total[:seen, :rank] += dot_nn(weights[step, :seen, :], grads[own, :])

        for steps in range(1, half // STEP + 1):
            pl.when(visible_steps == steps)(functools.partial(run_of_queries, steps))

    place_rows(places, total, kept, me & 1, ctx_axis)


def query_grad_kernel(heads, tokens, pieces, places, score_grads, keys, cosine, sine, *refs):
    before, refs = refs[:-5], refs[-5:]
    d_latent, d_rope, by_head, stage, done = refs
    me = lax.axis_index("ctx")
    rank, rope = stage.shape[1], cosine.shape[1]
    rows = RUN * heads
    span = TILE // heads
    to_heads = rows_to_heads(heads)

    def store(index):
        return pltpu.make_async_copy(
            stage.at[pl.ds(index * WIDE, WIDE)],
            d_latent.at[pl.ds(pieces[index] * WIDE, WIDE)],
            done.at[index],
        )

    def multiply(group, steps):
        seen = steps * STEP
        seen_keys = keys[:, :seen, :].reshape(2 * seen, keys.shape[2])
        for index in group:
            step, column = divmod(pieces[index] * WIDE, rows)
            grads = score_grads[step, :, :seen, column : column + WIDE].reshape(2 * seen, WIDE)
            value = dot_tn(grads, seen_keys)
            stage[index * WIDE : (index + 1) * WIDE, :] = value[:, :rank].astype(BF16)
            for tile in range(WIDE // TILE):
                here = slice(tile * TILE, (tile + 1) * TILE)
                start = (pieces[index] * WIDE + tile * TILE) // heads
                to = start - pieces[0] * WIDE // heads
                spread = lambda table: jnp.broadcast_to(
                    table[start : start + span, :][:, None, :], (span, heads, rope)
                ).reshape(TILE, rope)
                turned = value[here, rank : rank + rope]
                turned = (turned * spread(cosine) - half_turn_last(turned) * spread(sine)).astype(BF16)
                by_head[:, to : to + span, :] = dot_nn(to_heads, turned).reshape(heads, span, rope)

    for step in range(tokens // RUN):
        group = [index for index, piece in enumerate(pieces) if piece * WIDE // rows == step]
        if not group:
            continue
        first = places[me * tokens + step * RUN]
        visible_steps = ((first // RUN) * (RUN // 2)) // STEP + 1
        for steps in range(1, keys.shape[1] // STEP + 1):
            pl.when(visible_steps == steps)(functools.partial(multiply, group, steps))
        for index in group:
            store(index).start()
    if before:
        for head in range(heads):
            d_rope[head] = jnp.concatenate([before[1][head], by_head[head]], 0).T.astype(BF16)
    else:
        d_rope[...] = by_head[...]
    for index in range(len(pieces)):
        store(index).wait()


def pair_sum_kernel(kept, received, own, *others):
    own[...] = kept[0].astype(F32) + received[0].astype(F32)
    for chip, out in enumerate(others):
        out[...] = (kept[chip + 1].astype(F32) + received[chip + 1].astype(F32)).astype(BF16)


def plane_sum_kernel(own, *refs):
    head_axis = own.shape[0]
    received, kept, others = refs[: -head_axis], refs[-head_axis], refs[1 - head_axis :]
    mine = lax.axis_index("head")
    for far in range(head_axis):
        value = own[mine ^ far]
        for part in received:
            value += part[mine ^ far].astype(F32)
        if far == 0:
            kept[...] = value
        else:
            others[far - 1][...] = value.astype(BF16)


def head_sum_kernel(own, *refs):
    received, cosine, sine, d_latent, d_rope = refs[:-4], *refs[-4:]
    rank = d_latent.shape[1]
    value = own[...]
    for part in received:
        value += part[...].astype(F32)
    d_latent[...] = value[:, :rank]
    turned = value[:, rank:]
    d_rope[...] = turned * cosine[...] - half_turn_last(turned) * sine[...]


def pair(values, distance, axis):
    count = lax.axis_size(axis)
    return lax.ppermute(values, axis, [(i, i ^ distance) for i in range(count)])


def body(q_latent, q_rope, latent, rope_key, positions, d_out, w_uv):
    tokens, heads, rank = q_latent.shape
    rope = rope_key.shape[1]
    value_width = d_out.shape[2]
    sequence = positions.shape[0]
    head_axis, ctx_axis = lax.axis_size("head"), lax.axis_size("ctx")
    out_rows = sequence // (head_axis * ctx_axis)
    half = sequence // 2
    width = rank + rope
    padded = -(-width // 128) * 128
    rows = tokens * heads
    runs = tokens // RUN
    run_rows = RUN * heads
    scaling = (NOPE + rope) ** -0.5
    inverse = ROPE_BASE ** (-(np.arange(rope // 2, dtype=np.float64) / (rope // 2)))
    inverse = jnp.asarray(np.tile(inverse[:, None], (1, tokens)).astype(np.float32))

    def shape(*dims, dtype=BF16):
        return jax.ShapeDtypeStruct(dims, dtype)

    def cost(flops, nbytes, more=0):
        return pl.CostEstimate(flops=flops, bytes_accessed=nbytes, transcendentals=more)

    own_keys, tables = pl.pallas_call(
        functools.partial(key_kernel, head_axis, ctx_axis, out_rows),
        out_shape=(shape(tokens, width), shape(3, rope // 2, tokens, dtype=F32)),
        in_specs=[smem(), vmem(), vmem(), vmem()],
        out_specs=(vmem(),) * 2,
        compiler_params=params(58),
        cost_estimate=cost(8 << 30, 32 * MIB),
        name="own_keys",
    )(positions, latent, rope_key.T, inverse)

    blocks = [own_keys] + [None] * (ctx_axis - 1)
    for chip in range(1, ctx_axis // 2):
        blocks[2 * chip] = pair(own_keys, 2 * chip, "ctx")

    query_rows, grad_rows, own_cosine, own_sine, out_cosine, out_sine = pl.pallas_call(
        functools.partial(query_kernel, heads),
        out_shape=(shape(rows, padded), shape(rows, rank))
        + (shape(tokens, rope, dtype=F32),) * 2
        + (shape(out_rows, rope, dtype=F32),) * 2,
        in_specs=[vmem()] * 5,
        out_specs=(vmem(),) * 6,
        scratch_shapes=[
            pltpu.VMEM((heads, tokens, value_width), BF16),
            pltpu.VMEM((heads, tokens, width), BF16),
        ],
        compiler_params=params(24),
        cost_estimate=cost(2 * rows * rank * value_width, 10 * MIB),
        name="query_rows",
    )(
        q_latent.reshape(rows, rank),
        q_rope.transpose(1, 2, 0),
        d_out.reshape(rows, value_width),
        w_uv,
        tables,
    )

    blocks, query_rows, grad_rows = lax.optimization_barrier((blocks[::2], query_rows, grad_rows))
    blocks = [block for chip in blocks for block in (chip, pair(chip, 1, "ctx"))]

    slots = (ctx_axis // 2, head_axis, out_rows, width)
    sent, keys, weights_kept, score_grads = pl.pallas_call(
        functools.partial(front_kernel, ctx_axis, heads, tokens, out_rows, scaling),
        out_shape=(
            shape(*slots),
            shape(2, half, padded),
            shape(runs, half, run_rows),
            shape(runs, 2, half, run_rows),
        ),
        in_specs=[smem()] + [vmem()] * (ctx_axis + 2),
        out_specs=(vmem(),) * 4,
        scratch_shapes=[
            pltpu.VMEM((half, run_rows), BF16),
            pltpu.VMEM((half, padded), F32),
            pltpu.VMEM((2, sequence, TILE), F32),
            pltpu.VMEM((2, sequence, TILE), F32),
        ],
        compiler_params=params(30),
        cost_estimate=cost(7 * rows * sequence * width, 20 * MIB),
        name="front",
    )(positions, *blocks, query_rows, grad_rows)

    received = pair(sent, 1, "ctx")

    kept = pl.pallas_call(
        functools.partial(key_grad_kernel, ctx_axis, heads, tokens),
        out_shape=shape(*slots),
        in_specs=[smem()] + [vmem()] * 4,
        out_specs=vmem(),
        scratch_shapes=[pltpu.VMEM((half, padded), F32)],
        compiler_params=params(20),
        cost_estimate=cost(2 * rows * sequence * width, 10 * MIB),
        name="key_grad",
    )(positions, weights_kept, score_grads, query_rows, grad_rows)

    def small(kernel, outs, *operands):
        return pl.pallas_call(
            kernel,
            out_shape=outs,
            in_specs=[vmem()] * len(operands),
            out_specs=(vmem(),) * len(outs),
            compiler_params=params(4),
            name=kernel.__name__,
        )(*operands)

    low, high = shape(*slots[1:]), shape(*slots[1:], dtype=F32)
    own, *others = small(pair_sum_kernel, (high,) + (low,) * (slots[0] - 1), kept, received)
    others = [pair(part, 2 * (chip + 1), "ctx") for chip, part in reversed(list(enumerate(others)))]

    anywhere = pl.BlockSpec(memory_space=pl.ANY)

    def query_grad(pieces, *before):
        part = shape(heads, len(pieces) * WIDE // heads, rope, dtype=F32)
        return pl.pallas_call(
            functools.partial(query_grad_kernel, heads, tokens, pieces),
            out_shape=(shape(rows, rank), shape(heads, rope, tokens) if before else part),
            in_specs=[smem()] + [vmem()] * 4 + [anywhere, vmem()] * bool(before),
            out_specs=(anywhere, vmem()),
            input_output_aliases={5: 0} if before else {},
            scratch_shapes=[
                pltpu.VMEM(part.shape, F32),
                pltpu.VMEM((len(pieces) * WIDE, rank), BF16),
                pltpu.SemaphoreType.DMA((len(pieces),)),
            ],
            compiler_params=params(20),
            cost_estimate=cost(2 * len(pieces) * WIDE * sequence * width, 5 * MIB),
            name="query_grad",
        )(positions, score_grads, keys, own_cosine, own_sine, *before)

    pieces = range(rows // WIDE)
    d_q_latent, turned = query_grad(pieces[:-1])
    others, d_q_latent, turned = lax.optimization_barrier((others, d_q_latent, turned))
    low, high = shape(*slots[2:]), shape(*slots[2:], dtype=F32)
    own, *others = small(plane_sum_kernel, (high,) + (low,) * (head_axis - 1), own, *others)
    others, d_q_latent, turned = lax.optimization_barrier((others, d_q_latent, turned))
    others = [pair(part, far + 1, "head") for far, part in reversed(list(enumerate(others)))]
    d_q_latent, d_q_rope = query_grad(pieces[-1:], d_q_latent, turned)
    others, d_q_latent, d_q_rope = lax.optimization_barrier((others, d_q_latent, d_q_rope))
    d_latent, d_rope_key = small(
        head_sum_kernel,
        (shape(out_rows, rank, dtype=F32), shape(out_rows, rope, dtype=F32)),
        own,
        *others,
        out_cosine,
        out_sine,
    )
    return (
        d_q_latent.reshape(tokens, heads, rank),
        d_q_rope.transpose(2, 0, 1),
        d_latent,
        d_rope_key,
    )


def solution(mesh):
    placed = (
        P("ctx", "head", None),
        P("ctx", "head", None),
        P("ctx", None),
        P("ctx", None),
        P(),
        P("ctx", "head", None),
        P("head", None, None),
    )
    return jax.shard_map(
        body,
        mesh=mesh,
        in_specs=placed,
        out_specs=(
            P("ctx", "head", None),
            P("ctx", "head", None),
            P(("head", "ctx"), None),
            P(("head", "ctx"), None),
        ),
        check_vma=False,
    )
```
